32 devices in a mesh: wake: 16 (over z, y, core), col: 2 (over x).
Axes of the slice: x: 2, y: 2, z: 4, core: 2. Of those that a mesh axis runs over, the one named last changes fastest.
Arguments:
- points: float32 [3, 32768], P(None, ('wake', 'col')), may hold values from -6 to 6
- normals: float32 [3, 32768], P(None, ('wake', 'col')), may hold values from -6 to 6
- freestream: float32 [3], replicated, may hold values from -2 to 2
- wake_nodes: float32 [3, 16384], P(None, 'wake'), may hold values from -6 to 6
- circulation: float32 [16384], P('wake'), may hold values from -4 to 4
- filament: int32 [16384], P('wake'), may hold values from 0 to 127, never falling along the last dimension, each value on 1 to 256 neighbouring positions
- self_term: float32 [32768], P(('wake', 'col')), may hold values from 1 to 8
- near_blocks: float32 [256, 2, 1, 128, 128], P('wake', 'col'), may hold values from -0.5 to 0.5
- near_index: int32 [256, 2, 1], P('wake', 'col'), may hold values from 0 to 127
- far_left: float32 [2, 32, 32768], P('col', None, 'wake'), may hold values from -1 to 1
- far_right: float32 [16, 32, 32768], P('wake', None, 'col'), may hold values from -0.046875 to 0.046875
Outputs:
- right_side: float32 [32768], P(('wake', 'col'))
- strengths: float32 [32768], P(('wake', 'col'))
The draws below stay inside these ranges and needn't reach their ends.
Inputs may be any that keep to these rules, and one draw needn't show every extreme that they name: Filament numbers never fall along the nodes; each filament has 1 to 256 nodes and one has exactly 256.
All inputs are finite; a program needn't handle non-finite values.
Results may differ from the reference program's by a relative error of at most 0.0004.
Values sent between devices are 32-bit elements; how exact they have to be, the bound alone decides.
No kernel may reach another device: no remote copies, remote signals or barrier semaphores. Data moves between devices by JAX's collectives and lax.ppermute only.
A program may use at most 64 MiB of HBM per device.

```python
import math
import jax
import jax.numpy as jnp
import numpy as np
from jax import lax

BLOCK = 128
RANK = 32
NEAR = 1
KRYLOV = 6
FIL_LEN = 256
R_DEV = 2048
NP = 32768
COLS = 16384
NODES = 16384
FILAMENTS = 128
N_WAKE = 16
N_COL = 2


def draw_normals(key, part):
    group_rank = jax.random.permutation(jax.random.fold_in(key, 11), N_COL)
    group_level = jnp.power(10.0, -group_rank.astype(jnp.float32))
    panel_group = jnp.arange(NP, dtype=jnp.int32) // (R_DEV // N_COL) % N_COL
    panel_level = group_level[panel_group]
    raw_values = jax.random.normal(jax.random.fold_in(key, 13), (3, NP), jnp.float32)
    return jnp.clip(raw_values * panel_level[None, :], -6.0, 6.0)


def draw_self_term(key, part):
    upper_mode = jax.random.bernoulli(jax.random.fold_in(key, 17), 0.5, (NP,))
    uniform_draw = jax.random.uniform(jax.random.fold_in(key, 19), (NP,), jnp.float32)
    lower_values = 1.0 + 0.5 * uniform_draw
    upper_values = 6.0 + 2.0 * uniform_draw
    return jnp.where(upper_mode, upper_values, lower_values)


def plant(result, key, smallest, largest):
    longest = result.shape.index(max(result.shape))
    spots = []
    for shift in (0, 1):
        where = [jax.random.randint(jax.random.fold_in(key, axis), (), 0, length) for axis, length in enumerate(result.shape)]
        where[longest] = (where[longest] + shift) % result.shape[longest]
        spots.append(tuple(where))
    return result.at[spots[0]].set(smallest).at[spots[1]].set(largest)


def level_of(own_key, shape, shards, least, top_value):
    gain, own = 1.0, jax.random.fold_in(own_key, 6)
    for dim, blocks in shards:
        draws = jnp.exp(jax.random.uniform(jax.random.fold_in(own, dim), (blocks,), jnp.float32, least / len(shards), top_value / len(shards)))
        gain = gain * jnp.repeat(draws, shape[dim] // blocks).reshape([-1 if axis == dim else 1 for axis in range(len(shape))])
    return gain


def length_profile(count, total, reach, slope):
    loads = [(1 << 20) // math.isqrt(grade ** slope) + 1 for grade in range(2, count + 1)]
    surplus, counts = total - reach - (count - 1), [1] * (count - 1)
    while surplus > 0:
        free = [i for i in range(count - 1) if counts[i] < reach]
        whole, budget = sum([loads[i] for i in free]), surplus
        for i in free:
            addition = min(reach - counts[i], max(1, budget * loads[i] // whole), surplus)
            counts[i] = counts[i] + addition
            surplus = surplus - addition
    return np.array([reach] + counts)


def uneven_parts(stream_key, number_of, total, most, lean):
    if number_of == 2:
        one = jax.random.randint(stream_key, (), max(1, total - most), min(most, total - 1) + 1)
        return jnp.stack([one, total - one])
    tallies = jnp.asarray(length_profile(number_of, total, most, lean), jnp.int32)
    pairs = (number_of - 1) // 2
    source_of, taker = tallies[1:1 + 2 * pairs:2], tallies[2:2 + 2 * pairs:2]
    room = jnp.minimum(source_of - 1, most - taker)
    moved = jax.random.randint(jax.random.fold_in(stream_key, 1), (pairs,), 0, 1 << 20) % (room + 1)
    tallies = tallies.at[1:1 + 2 * pairs:2].set(source_of - moved).at[2:2 + 2 * pairs:2].set(taker + moved)
    return tallies[jax.random.permutation(jax.random.fold_in(stream_key, 2), number_of)]


def scatter_about(own_key, dims, spread, reach, cuts=(), held_as=jnp.bfloat16):
    drawn = jax.random.normal(own_key, dims, jnp.float32) * spread
    if len(cuts) > 0:
        drawn = level_of(own_key, dims, cuts, -0.22, 0.18) * drawn
    return jnp.clip(drawn, min=-reach, max=reach).astype(held_as)


def setup_inputs(seed: int = 0) -> dict:
    splits = jax.random.split(jax.random.key(seed), 12)
    return {
        "points": scatter_about(splits[0], (3, NP), 1.0, 6.0, ((1, 32),), jnp.float32),
        "normals": draw_normals(jax.random.fold_in(splits[11], 71), 0),
        "freestream": jnp.clip(jax.random.uniform(splits[2], (3,), jnp.float32, -2.0, 2.0), -2.0, 2.0),
        "wake_nodes": scatter_about(splits[3], (3, NODES), 1.0, 6.0, ((1, 16),), jnp.float32),
        "circulation": scatter_about(splits[4], (NODES,), 0.5, 4.0, ((0, 16),), jnp.float32),
        "filament": jnp.searchsorted(jnp.cumsum(uneven_parts(splits[5], FILAMENTS, NODES, FIL_LEN, 0)), jnp.arange(NODES), side="right").astype(jnp.int32),
        "self_term": draw_self_term(jax.random.fold_in(splits[11], 71), 0),
        "near_blocks": scatter_about(splits[7], (NP // BLOCK, N_COL, NEAR, BLOCK, BLOCK), (0.6 / (N_COL * NEAR * BLOCK) ** 0.5), 0.5, ((0, 16), (1, 2)), jnp.float32),
        "near_index": plant(jax.random.randint(splits[8], (NP // BLOCK, N_COL, NEAR), 0, COLS // BLOCK), jax.random.fold_in(splits[8], 1), 0, (COLS // BLOCK) - 1).astype(jnp.int32),
        "far_left": scatter_about(splits[9], (N_COL, RANK, NP), (0.5 / (RANK * N_COL) ** 0.5), 1.0, ((0, 2), (2, 16)), jnp.float32),
        "far_right": scatter_about(splits[10], (N_WAKE, RANK, NP), COLS ** -0.5, 0.046875, ((0, 16), (2, 2)), jnp.float32),
    }


core_sq = 0.01
four_pi = 4.0 * math.pi

def induce(points, normals, segments):
    near_arm = points[:, :, None] - segments[0:3, None, :]
    far_arm = points[:, :, None] - segments[3:6, None, :]
    cross_x = near_arm[1] * far_arm[2] - near_arm[2] * far_arm[1]
    cross_y = near_arm[2] * far_arm[0] - near_arm[0] * far_arm[2]
    cross_z = near_arm[0] * far_arm[1] - near_arm[1] * far_arm[0]
    normal_part = cross_x * normals[0][:, None] + cross_y * normals[1][:, None] + cross_z * normals[2][:, None]
    near_len = jnp.sqrt(lax.optimization_barrier(jnp.sum(near_arm * near_arm, axis=0)))
    far_len = jnp.sqrt(lax.optimization_barrier(jnp.sum(far_arm * far_arm, axis=0)))
    inner_dot = lax.optimization_barrier(jnp.sum(near_arm * far_arm, axis=0))
    factor = segments[6][None, :] * (near_len + far_len) / (four_pi * (near_len * far_len * (near_len * far_len + inner_dot) + core_sq))
    return lax.optimization_barrier(jnp.sum(factor * normal_part, axis=1))

def small_solve(gram_matrix, projected):
    size_now = gram_matrix.shape[0]
    factor = [[None for inner_pos in range(size_now)] for outer_pos in range(size_now)]
    for outer_pos in range(size_now):
        for inner_pos in range(outer_pos + 1):
            partial_sum = gram_matrix[outer_pos, inner_pos]
            for middle in range(inner_pos):
                partial_sum = partial_sum - factor[outer_pos][middle] * factor[inner_pos][middle]
            if inner_pos == outer_pos:
                factor[outer_pos][inner_pos] = jnp.sqrt(partial_sum)
            else:
                factor[outer_pos][inner_pos] = partial_sum / factor[inner_pos][inner_pos]
    forward = []
    for outer_pos in range(size_now):
        partial_sum = projected[outer_pos]
        for middle in range(outer_pos):
            partial_sum = partial_sum - factor[outer_pos][middle] * forward[middle]
        forward.append(partial_sum / factor[outer_pos][outer_pos])
    backward = [None for outer_pos in range(size_now)]
    for outer_pos in reversed(range(size_now)):
        partial_sum = forward[outer_pos]
        for middle in range(outer_pos + 1, size_now):
            partial_sum = partial_sum - factor[middle][outer_pos] * backward[middle]
        backward[outer_pos] = partial_sum / factor[outer_pos][outer_pos]
    return backward

def apply_operator(vector, self_term, near_blocks, near_index, far_left, far_right):
    highest = lax.Precision.HIGHEST
    piece_len = R_DEV // N_COL
    column_vec = vector.reshape(N_WAKE, N_COL, piece_len).transpose(1, 0, 2).reshape(N_COL, COLS)
    far_coeff = jnp.einsum('wkcn,cn->wck', far_right.reshape(N_WAKE, RANK, N_COL, COLS), column_vec, precision=highest)
    far_part = jnp.einsum('ckwr,wck->wr', far_left.reshape(N_COL, RANK, N_WAKE, R_DEV), far_coeff, precision=highest).reshape(NP)
    column_blocks = column_vec.reshape(N_COL, COLS // BLOCK, BLOCK)
    group_ids = jnp.arange(N_COL, dtype=jnp.int32)[None, :, None]
    selected = column_blocks[group_ids, near_index]
    near_part = jnp.einsum('rckij,rckj->ri', near_blocks, selected, precision=highest).reshape(NP)
    return self_term * vector + near_part + far_part

def reference(points, normals, freestream, wake_nodes, circulation, filament, self_term, near_blocks, near_index, far_left, far_right):
    highest = lax.Precision.HIGHEST
    filament_tag = filament.astype(jnp.float32) + 1.0
    next_tag = jnp.concatenate([filament_tag[1:], jnp.zeros((1,), jnp.float32)])
    link_mask = (filament_tag == next_tag).astype(jnp.float32)
    end_points = jnp.concatenate([wake_nodes[:, 1:], jnp.zeros((3, 1), jnp.float32)], axis=1)
    segments = jnp.concatenate([wake_nodes, end_points, (circulation * link_mask)[None, :]], axis=0)
    panel_block = math.gcd(NP, 256)
    point_groups = points.reshape(3, NP // panel_block, panel_block).transpose(1, 0, 2)
    normal_groups = normals.reshape(3, NP // panel_block, panel_block).transpose(1, 0, 2)
    induced = lax.map(lambda member_pair: induce(member_pair[0], member_pair[1], segments), (point_groups, normal_groups)).reshape(NP)
    right_side = -(jnp.dot(freestream, normals, precision=highest) + induced)
    initial_norm = jnp.sqrt(jnp.sum(right_side * right_side))
    krylov = [right_side / initial_norm]
    hessenberg = jnp.zeros((KRYLOV + 1, KRYLOV), jnp.float32)
    for column in range(KRYLOV):
        image_vec = apply_operator(krylov[column], self_term, near_blocks, near_index, far_left, far_right)
        coeffs = jnp.stack([jnp.sum(image_vec * member) for member in krylov])
        remainder = image_vec
        for position in range(column + 1):
            remainder = remainder - coeffs[position] * krylov[position]
        new_norm = jnp.sqrt(jnp.sum(remainder * remainder))
        hessenberg = hessenberg.at[:column + 1, column].set(coeffs).at[column + 1, column].set(new_norm)
        krylov.append(remainder / new_norm)
    gram_matrix = jnp.dot(hessenberg.T, hessenberg, precision=highest)
    combination = small_solve(gram_matrix, initial_norm * hessenberg[0])
    strengths = combination[0] * krylov[0]
    for position in range(1, KRYLOV):
        strengths = strengths + combination[position] * krylov[position]
    return (right_side, strengths)
```

```python
import functools
import math

import jax
import jax.numpy as jnp
from jax import lax
from jax.experimental import pallas as pl
from jax.experimental.pallas import tpu as pltpu
from jax.sharding import PartitionSpec as P

KRYLOV = 6
CORE_SQ = 0.01
FOUR_PI = 4.0 * math.pi
LANES = 128
FEATURES = 48
PIECE_OF_PANEL = (0, 0, 1, 0, 2, 1)
PIECE_OF_SEGMENT = (0, 1, 0, 2, 0, 1)
PANEL_STEP = 64
NODE_STEP = 16

VMEM = pl.BlockSpec(memory_space=pltpu.VMEM)
SMEM = pl.BlockSpec(memory_space=pltpu.SMEM)


def three_pieces(value):
    high = value.astype(jnp.bfloat16).astype(jnp.float32)
    rest = value - high
    middle = rest.astype(jnp.bfloat16).astype(jnp.float32)
    low = (rest - middle).astype(jnp.bfloat16).astype(jnp.float32)
    return high, middle, low


def pack_kernel(nodes_ref, circulation_ref, filament_ref, out_ref):
    copies, _, rows, _ = out_ref.shape
    own = [
        jnp.concatenate([nodes_ref[q : q + 1, r * LANES : (r + 1) * LANES] for r in range(rows)], axis=0)
        for q in range(3)
    ]
    own.append(circulation_ref[...])
    own.append(filament_ref[...].astype(jnp.float32) + 1.0)
    for q in range(5):
        for k in range(copies):
            out_ref[k, q] = own[q]


def pack_nodes(wake_nodes, circulation, filament, copies):
    rows = circulation.shape[0] // LANES
    return pl.pallas_call(
        pack_kernel,
        out_shape=jax.ShapeDtypeStruct((copies, 5, rows, LANES), jnp.float32),
        in_specs=[VMEM, VMEM, VMEM],
        out_specs=VMEM,
        name="pack_nodes",
    )(wake_nodes, circulation.reshape(rows, LANES), filament.reshape(rows, LANES))


def induce_kernel(
    nodes_ref, points_ref, normals_ref, stream_ref, right_ref, copies_ref,
    row_ref, feature_ref, feature_bf_ref, panel_ref, panel_bf_ref, total_ref,
):
    rows = nodes_ref.shape[0] * nodes_ref.shape[2]
    x, y, z, circulation, tag = [nodes_ref[:, q].reshape(rows, LANES) for q in range(5)]
    piece_rows = right_ref.shape[0]

    def spread(ref, q):
        return jnp.concatenate(
            [ref[q : q + 1, r * LANES : (r + 1) * LANES] for r in range(piece_rows)], axis=0
        )

    points = [spread(points_ref, q) for q in range(3)]
    normals = [spread(normals_ref, q) for q in range(3)]
    middle = [0.5 * (jnp.max(p, keepdims=True) + jnp.min(p, keepdims=True)) for p in points]

    px, py, pz = [points[q] - middle[q] for q in range(3)]
    panel_features = [
        normals[1] * pz - normals[2] * py,
        normals[2] * px - normals[0] * pz,
        normals[0] * py - normals[1] * px,
        normals[0], normals[1], normals[2],
    ]
    panel_pieces = [three_pieces(feature) for feature in panel_features]
    for r in range(piece_rows):
        own = slice(r * LANES, (r + 1) * LANES)
        for q in range(3):
            panel_ref[q, own, :] = jnp.broadcast_to(points[q][r : r + 1, :], (LANES, LANES)).T
        stack = jnp.concatenate(
            [panel_pieces[k][p][r : r + 1, :] for p in PIECE_OF_PANEL for k in range(6)]
            + [jnp.zeros((LANES - 36, LANES), jnp.float32)],
            axis=0,
        )
        panel_bf_ref[own, :] = stack.T[:, :FEATURES].astype(jnp.bfloat16)

    lane = lax.broadcasted_iota(jnp.int32, (rows, LANES), 1)
    row = lax.broadcasted_iota(jnp.int32, (rows, LANES), 0)

    def following(value):
        turned = pltpu.roll(value, LANES - 1, 1)
        return jnp.where(lane == LANES - 1, pltpu.roll(turned, rows - 1, 0), turned)

    nx, ny, nz, next_tag = [following(value) for value in (x, y, z, tag)]
    linked = (tag == next_tag) & ((lane < LANES - 1) | (row < rows - 1))
    strength = jnp.where(linked, circulation * (1.0 / FOUR_PI), 0.0)
    ex, ey, ez = x - nx, y - ny, z - nz
    ax, ay, az = x - middle[0], y - middle[1], z - middle[2]
    bx, by, bz = nx - middle[0], ny - middle[1], nz - middle[2]
    segment_features = [
        strength * ex, strength * ey, strength * ez,
        strength * (ay * bz - az * by),
        strength * (az * bx - ax * bz),
        strength * (ax * by - ay * bx),
    ]
    total_ref[...] = jnp.zeros_like(total_ref)
    feature_ref[...] = jnp.zeros_like(feature_ref)
    for group in range(rows // LANES):
        own = slice(group * LANES, (group + 1) * LANES)
        for q, value in enumerate((x, y, z)):
            row_ref[q, 0:LANES, :] = value[own].T
        for q, value in enumerate((nx, ny, nz)):
            row_ref[q, LANES : LANES + 8, :] = jnp.broadcast_to(value[own].T[LANES - 1 : LANES], (8, LANES))
        for k in range(6):
            pieces = three_pieces(segment_features[k][own].T)
            for p in range(6):
                feature_ref[pl.ds(p * 6 + k, LANES, stride=FEATURES), :] = pieces[PIECE_OF_SEGMENT[p]]

        def narrow(i, carry):
            part = pl.ds(pl.multiple_of(i * FEATURES, FEATURES), FEATURES)
            feature_bf_ref[part, :] = feature_ref[part, :].astype(jnp.bfloat16)
            return carry

        lax.fori_loop(0, LANES, narrow, 0, unroll=8)

        def arms(panel, t):
            rx, ry, rz = [panel[q] - row_ref[q, pl.ds(t, 1), :] for q in range(3)]
            square = rx * rx + ry * ry + rz * rz
            return rx, ry, rz, square * lax.rsqrt(jnp.maximum(square, 1e-36))

        def panel_step(b, carry):
            part = pl.ds(pl.multiple_of(b * PANEL_STEP, PANEL_STEP), PANEL_STEP)
            panel = [panel_ref[q, part, :] for q in range(3)]
            features = panel_bf_ref[part, :]

            def node_step(block, state):
                (rx, ry, rz, length), total = state
                first = pl.multiple_of(block * NODE_STEP, NODE_STEP)
                base = pl.multiple_of(first * FEATURES, FEATURES)
                for k in range(NODE_STEP):
                    normal_part = jnp.dot(
                        features,
                        feature_bf_ref[pl.ds(base + k * FEATURES, FEATURES), :],
                        preferred_element_type=jnp.float32,
                    )
                    sx, sy, sz, after = arms(panel, first + k + 1)
                    product = length * after
                    inner = rx * sx + ry * sy + rz * sz
                    below = product * (product + inner) + CORE_SQ
                    total = total + ((length + after) * normal_part) * pl.reciprocal(below)
                    rx, ry, rz, length = sx, sy, sz, after
                return (rx, ry, rz, length), total

            start = (arms(panel, 0), jnp.zeros((PANEL_STEP, LANES), jnp.float32))
            _, total = lax.fori_loop(0, LANES // NODE_STEP, node_step, start)
            total_ref[part, :] += total
            return carry

        lax.fori_loop(0, piece_rows * LANES // PANEL_STEP, panel_step, 0)

    onset = stream_ref[0] * normals[0] + stream_ref[1] * normals[1] + stream_ref[2] * normals[2]
    for r in range(piece_rows):
        induced = jnp.sum(total_ref[r * LANES : (r + 1) * LANES, :].T, axis=0, keepdims=True)
        right_ref[r : r + 1, :] = -(onset[r : r + 1, :] + induced)
    right = right_ref[...]
    for k in range(copies_ref.shape[0]):
        copies_ref[k] = right


def induce(nodes, points, normals, freestream, copies):
    piece = points.shape[1]
    piece_rows = piece // LANES
    pairs = piece * nodes.size // 5
    return pl.pallas_call(
        induce_kernel,
        out_shape=(
            jax.ShapeDtypeStruct((piece_rows, LANES), jnp.float32),
            jax.ShapeDtypeStruct((copies, piece_rows, LANES), jnp.float32),
        ),
        in_specs=[VMEM, VMEM, VMEM, SMEM],
        out_specs=(VMEM, VMEM),
        scratch_shapes=[
            pltpu.VMEM((3, LANES + 8, LANES), jnp.float32),
            pltpu.VMEM((LANES * FEATURES, LANES), jnp.float32),
            pltpu.VMEM((LANES * FEATURES, LANES), jnp.bfloat16),
            pltpu.VMEM((3, piece, LANES), jnp.float32),
            pltpu.VMEM((piece, FEATURES), jnp.bfloat16),
            pltpu.VMEM((piece, LANES), jnp.float32),
        ],
        compiler_params=pltpu.CompilerParams(vmem_limit_bytes=24 * 2**20),
        cost_estimate=pl.CostEstimate(flops=30 * pairs, bytes_accessed=2**21, transcendentals=2 * pairs),
        name="induce",
    )(nodes, points, normals, freestream)


def whole_sum(value):
    return jnp.sum(value, keepdims=True)


def orthogonalize(image_ref, known_refs, column_ref):
    image = image_ref[...].reshape(-1, LANES)
    known = [ref[...] for ref in known_refs]
    coeffs = [whole_sum(image * member) for member in known]
    for coeff, member in zip(coeffs, known):
        image = image - coeff * member
    norm = jnp.sqrt(whole_sum(image * image))
    for i, value in enumerate(coeffs + [norm]):
        column_ref[i : i + 1, :] = jnp.broadcast_to(value, (1, LANES))
    return image / norm


def step_kernel(known_count, n_col, *refs):
    place_ref, index_refs, refs = refs[0], refs[1 : 1 + n_col], refs[1 + n_col :]
    image_ref, known_refs, refs = refs[0], refs[1 : 1 + known_count], refs[1 + known_count :]
    self_ref, refs = refs[0], refs[1:]
    near_refs, left_refs, right_refs = refs[:n_col], refs[n_col : 2 * n_col], refs[2 * n_col : 3 * n_col]
    vector_ref, column_ref, copies_ref = refs[3 * n_col :]
    piece_rows = self_ref.shape[0]
    piece = piece_rows * LANES
    rank = right_refs[0].shape[0]
    n_wake = right_refs[0].shape[1] // piece
    vector_ref[...] = orthogonalize(image_ref, known_refs, column_ref)
    place, mine = place_ref[0], place_ref[1]

    far = jnp.zeros((rank, piece), jnp.float32)
    near = [jnp.zeros((LANES, LANES), jnp.float32) for _ in range(piece_rows)]
    for shift in range(n_col):
        group = lax.rem(mine - shift + n_col, n_col)

        def chunk(w, total):
            first = (w * n_col + group) * piece_rows
            for r in range(piece_rows):
                entries = vector_ref[pl.ds(first + r, 1), :]
                columns = pl.ds(pl.multiple_of(w * piece, LANES) + r * LANES, LANES)
                total = total + right_refs[shift][:, columns] * entries
            return total

        coeff = lax.fori_loop(0, n_wake, chunk, jnp.zeros((rank, LANES), jnp.float32), unroll=4)
        coeff = jnp.sum(coeff, axis=1, keepdims=True)
        if shift == 0:
            left = left_refs[0][:, pl.ds(pl.multiple_of(mine * piece, LANES), piece)]
        else:
            left = left_refs[shift][...]
        far = far + left * coeff
        for r in range(piece_rows):
            if shift == 0:
                row_block = mine * piece_rows + r
            else:
                row_block = r
            block = index_refs[shift][row_block if shift == 0 else r]
            where = (lax.div(block, piece_rows) * n_col + group) * piece_rows + lax.rem(block, piece_rows)
            near[r] = near[r] + near_refs[shift][row_block] * vector_ref[pl.ds(where, 1), :]
    far = jnp.sum(far, axis=0, keepdims=True)
    out_rows = []
    for r in range(piece_rows):
        out_rows.append(
            jnp.sum(near[r].T, axis=0, keepdims=True) + far[:, r * LANES : (r + 1) * LANES]
        )
    own = vector_ref[pl.ds(pl.multiple_of(place * piece_rows, piece_rows), piece_rows), :]
    image = self_ref[...] * own + jnp.concatenate(out_rows, axis=0)
    for k in range(copies_ref.shape[0]):
        copies_ref[k] = image


def arnoldi_step(place, indices, image, known, self_term, nears, lefts, rights):
    n_col = len(nears)
    copies, piece_rows, _ = image.shape
    total_rows = copies * piece_rows
    operands = [image, *known, self_term, *nears, *lefts, *rights]
    return pl.pallas_call(
        functools.partial(step_kernel, len(known), n_col),
        out_shape=(
            jax.ShapeDtypeStruct((total_rows, LANES), jnp.float32),
            jax.ShapeDtypeStruct((8, LANES), jnp.float32),
            jax.ShapeDtypeStruct((copies, piece_rows, LANES), jnp.float32),
        ),
        in_specs=[SMEM] * (1 + n_col) + [VMEM] * len(operands),
        out_specs=(VMEM, VMEM, VMEM),
        compiler_params=pltpu.CompilerParams(vmem_limit_bytes=32 * 2**20),
        name="arnoldi_step",
    )(place, *indices, *operands)


def small_solve(gram_matrix, projected):
    size_now = len(projected)
    factor = [[None for inner_pos in range(size_now)] for outer_pos in range(size_now)]
    for outer_pos in range(size_now):
        for inner_pos in range(outer_pos + 1):
            partial_sum = gram_matrix[outer_pos][inner_pos]
            for middle in range(inner_pos):
                partial_sum = partial_sum - factor[outer_pos][middle] * factor[inner_pos][middle]
            if inner_pos == outer_pos:
                factor[outer_pos][inner_pos] = jnp.sqrt(partial_sum)
            else:
                factor[outer_pos][inner_pos] = partial_sum / factor[inner_pos][inner_pos]
    forward = []
    for outer_pos in range(size_now):
        partial_sum = projected[outer_pos]
        for middle in range(outer_pos):
            partial_sum = partial_sum - factor[outer_pos][middle] * forward[middle]
        forward.append(partial_sum / factor[outer_pos][outer_pos])
    backward = [None for outer_pos in range(size_now)]
    for outer_pos in reversed(range(size_now)):
        partial_sum = forward[outer_pos]
        for middle in range(outer_pos + 1, size_now):
            partial_sum = partial_sum - factor[middle][outer_pos] * backward[middle]
        backward[outer_pos] = partial_sum / factor[outer_pos][outer_pos]
    return backward


def finish_kernel(place_ref, image_ref, *refs):
    known_refs, column_refs, out_ref, last_ref = refs[:KRYLOV], refs[KRYLOV : 2 * KRYLOV], refs[-2], refs[-1]
    orthogonalize(image_ref, known_refs, last_ref)
    norm = column_refs[0][0:1, :]
    columns = []
    for column, ref in enumerate(list(column_refs[1:]) + [last_ref]):
        columns.append([ref[i : i + 1, :] for i in range(column + 2)])
    gram = [
        [sum(columns[i][k] * columns[j][k] for k in range(j + 2)) for j in range(i + 1)]
        for i in range(KRYLOV)
    ]
    combination = small_solve(gram, [norm * columns[j][0] for j in range(KRYLOV)])
    piece_rows = out_ref.shape[0]
    part = pl.ds(pl.multiple_of(place_ref[0] * piece_rows, piece_rows), piece_rows)
    strengths = combination[0] * known_refs[0][part, :]
    for position in range(1, KRYLOV):
        strengths = strengths + combination[position] * known_refs[position][part, :]
    out_ref[...] = strengths


def finish(place, image, known, columns):
    piece_rows = image.shape[1]
    return pl.pallas_call(
        finish_kernel,
        out_shape=jax.ShapeDtypeStruct((piece_rows, LANES), jnp.float32),
        in_specs=[SMEM] + [VMEM] * (1 + len(known) + len(columns)),
        out_specs=VMEM,
        scratch_shapes=[pltpu.VMEM((8, LANES), jnp.float32)],
        compiler_params=pltpu.CompilerParams(vmem_limit_bytes=16 * 2**20),
        name="finish",
    )(place, image, *known, *columns)


def body(
    points,
    normals,
    freestream,
    wake_nodes,
    circulation,
    filament,
    self_term,
    near_blocks,
    near_index,
    far_left,
    far_right,
):
    everyone = ("wake", "col")
    n_wake, n_col = lax.axis_size("wake"), lax.axis_size("col")
    copies = n_wake * n_col
    piece = points.shape[1]
    piece_rows = piece // LANES
    mine = lax.axis_index("col")
    place = jnp.stack([lax.axis_index("wake") * n_col + mine, mine])

    near_own, index_own = near_blocks[:, 0, 0], near_index[:, 0, 0]
    left_own, right_own = far_left[0], far_right[0]
    nears, indices, lefts, rights = [near_own], [index_own], [left_own], [right_own]
    for shift in range(1, n_col):
        pairs = [(source, (source + shift) % n_col) for source in range(n_col)]
        target = lax.rem(mine + shift, n_col)
        index_part = lax.dynamic_slice_in_dim(index_own, target * piece_rows, piece_rows, 0).astype(jnp.float32)
        nears.append(
            lax.ppermute(lax.dynamic_slice_in_dim(near_own, target * piece_rows, piece_rows, 0), "col", pairs)
        )
        indices.append(lax.ppermute(index_part, "col", pairs).astype(jnp.int32))
        lefts.append(lax.ppermute(lax.dynamic_slice_in_dim(left_own, target * piece, piece, 1), "col", pairs))
        rights.append(lax.ppermute(right_own, "col", pairs))

    packed = pack_nodes(wake_nodes, circulation, filament, n_wake)
    nodes = lax.all_to_all(packed, "wake", 0, 0, tiled=True)
    right_side, image_copies = induce(nodes, points, normals, freestream, copies)
    own_self = self_term.reshape(piece_rows, LANES)
    known, columns = [], []
    for _ in range(KRYLOV):
        image = lax.all_to_all(image_copies, everyone, 0, 0, tiled=True)
        vector, column, image_copies = arnoldi_step(
            place, indices, image, known, own_self, nears, lefts, rights
        )
        known.append(vector)
        columns.append(column)
    image = lax.all_to_all(image_copies, everyone, 0, 0, tiled=True)
    strengths = finish(place, image, known, columns)
    return right_side.reshape(piece), strengths.reshape(piece)


def solution(mesh):
    in_specs = (
        P(None, ("wake", "col")),
        P(None, ("wake", "col")),
        P(),
        P(None, "wake"),
        P("wake"),
        P("wake"),
        P(("wake", "col")),
        P("wake", "col", None, None, None),
        P("wake", "col", None),
        P("col", None, "wake"),
        P("wake", None, "col"),
    )
    out_specs = (P(("wake", "col")), P(("wake", "col")))
    return jax.shard_map(body, mesh=mesh, in_specs=in_specs, out_specs=out_specs, check_vma=False)
```

```python
import functools
import math

import jax
import jax.numpy as jnp
from jax import lax
from jax.experimental import pallas as pl
from jax.experimental.pallas import tpu as pltpu
from jax.sharding import PartitionSpec as P

KRYLOV = 6
CORE_SQ = 0.01
FOUR_PI = 4.0 * math.pi
LANES = 128
PIECE_OF_PANEL = (0, 0, 1, 0, 2, 1)
PIECE_OF_SEGMENT = (0, 1, 0, 2, 0, 1)
NORMAL_ROWS = 48
LENGTH_ROWS = 32
WIDE = 2 * LANES
HALF = LANES // 2
PANEL_STEP = 128
NODE_STEP = 32

VMEM = pl.BlockSpec(memory_space=pltpu.VMEM)
SMEM = pl.BlockSpec(memory_space=pltpu.SMEM)


def pack_kernel(nodes_ref, circulation_ref, filament_ref, out_ref):
    copies, _, rows, _ = out_ref.shape
    own = [
        jnp.concatenate([nodes_ref[q : q + 1, r * LANES : (r + 1) * LANES] for r in range(rows)], axis=0)
        for q in range(3)
    ]
    own.append(circulation_ref[...])
    own.append(filament_ref[...].astype(jnp.float32) + 1.0)
    for q in range(5):
        for k in range(copies):
            out_ref[k, q] = own[q]


def pack_nodes(wake_nodes, circulation, filament, copies):
    rows = circulation.shape[0] // LANES
    return pl.pallas_call(
        pack_kernel,
        out_shape=jax.ShapeDtypeStruct((copies, 5, rows, LANES), jnp.float32),
        in_specs=[VMEM, VMEM, VMEM],
        out_specs=VMEM,
        name="pack_nodes",
    )(wake_nodes, circulation.reshape(rows, LANES), filament.reshape(rows, LANES))


def three_pieces(value):
    high = value.astype(jnp.bfloat16).astype(jnp.float32)
    rest = value - high
    middle = rest.astype(jnp.bfloat16).astype(jnp.float32)
    low = (rest - middle).astype(jnp.bfloat16).astype(jnp.float32)
    return high, middle, low


def panels_kernel(points_ref, normals_ref, stream_ref, normal_side_ref, length_side_ref, onset_ref, middle_ref):
    piece_rows = onset_ref.shape[0]

    def spread(ref, q):
        return jnp.concatenate(
            [ref[q : q + 1, r * LANES : (r + 1) * LANES] for r in range(piece_rows)], axis=0
        )

    points = [spread(points_ref, q) for q in range(3)]
    normals = [spread(normals_ref, q) for q in range(3)]
    middle = [0.5 * (jnp.max(p, keepdims=True) + jnp.min(p, keepdims=True)) for p in points]
    for q in range(3):
        middle_ref[q : q + 1, :] = jnp.broadcast_to(middle[q], (1, LANES))
    px, py, pz = [points[q] - middle[q] for q in range(3)]
    features = [
        normals[1] * pz - normals[2] * py,
        normals[2] * px - normals[0] * pz,
        normals[0] * py - normals[1] * px,
        normals[0], normals[1], normals[2],
    ]
    pieces = [three_pieces(feature) for feature in features]
    side = [pieces[k][p] for p in PIECE_OF_PANEL for k in range(6)]
    side += [jnp.zeros_like(px)] * (NORMAL_ROWS - len(side))
    pieces = [three_pieces(value) for value in (px, py, pz)]
    side += [pieces[k][p] for p in PIECE_OF_PANEL for k in range(3)]
    side += list(three_pieces(px * px + py * py + pz * pz)) + [jnp.ones_like(px)] * 3
    side += [jnp.zeros_like(px)] * (LANES - len(side))
    for r in range(piece_rows):
        own = slice(r * LANES, (r + 1) * LANES)
        turned = jnp.concatenate([value[r : r + 1, :] for value in side], axis=0).T
        normal_side_ref[own, :] = turned[:, :NORMAL_ROWS].astype(jnp.bfloat16)
        length_side_ref[own, :] = turned[:, NORMAL_ROWS : NORMAL_ROWS + LENGTH_ROWS].astype(jnp.bfloat16)
    onset_ref[...] = stream_ref[0] * normals[0] + stream_ref[1] * normals[1] + stream_ref[2] * normals[2]


def prepare_panels(points, normals, freestream):
    piece = points.shape[1]
    return pl.pallas_call(
        panels_kernel,
        out_shape=(
            jax.ShapeDtypeStruct((piece, NORMAL_ROWS), jnp.bfloat16),
            jax.ShapeDtypeStruct((piece, LENGTH_ROWS), jnp.bfloat16),
            jax.ShapeDtypeStruct((piece // LANES, LANES), jnp.float32),
            jax.ShapeDtypeStruct((8, LANES), jnp.float32),
        ),
        in_specs=[VMEM, VMEM, SMEM],
        out_specs=(VMEM, VMEM, VMEM, VMEM),
        name="prepare_panels",
    )(points, normals, freestream)


def induce_kernel(
    nodes_ref, normal_side_ref, length_side_ref, onset_ref, middle_ref, right_ref, copies_ref,
    normal_ref, length_ref, inner_ref, normal_bf_ref, length_bf_ref, inner_bf_ref, total_ref,
):
    rows = nodes_ref.shape[0] * nodes_ref.shape[2]
    groups = rows // LANES
    x, y, z, circulation, tag = [nodes_ref[:, q].reshape(rows, LANES) for q in range(5)]
    piece_rows = right_ref.shape[0]
    lane = lax.broadcasted_iota(jnp.int32, (rows, LANES), 1)
    row = lax.broadcasted_iota(jnp.int32, (rows, LANES), 0)
    turned = pltpu.roll(tag, LANES - 1, 1)
    next_tag = jnp.where(lane == LANES - 1, pltpu.roll(turned, rows - 1, 0), turned)
    linked = (tag == next_tag) & ((lane < LANES - 1) | (row < rows - 1))
    strength = jnp.where(linked, circulation * (1.0 / FOUR_PI), 0.0)
    runs = [
        [(value - middle_ref[q : q + 1, :])[g * LANES : (g + 1) * LANES].T for q, value in enumerate((x, y, z))]
        for g in range(groups)
    ]
    total_ref[...] = jnp.zeros_like(total_ref)
    last = lax.broadcasted_iota(jnp.int32, (1, LANES), 1) == LANES - 1
    ones = jnp.ones((HALF, LANES), jnp.float32)
    zeros = jnp.zeros((HALF, LANES), jnp.float32)

    def put(ref, size, offset, k, value):
        for half in range(2):
            ref[half, pl.ds(offset * size + k, HALF, stride=size), :] = value[half * HALF : (half + 1) * HALF]

    for k in range(36, NORMAL_ROWS):
        for half in range(2):
            normal_ref[half, pl.ds(k, HALF, stride=NORMAL_ROWS), :] = zeros
    for half in range(2):
        for k in range(24, LENGTH_ROWS):
            inner_ref[half, pl.ds(k, HALF, stride=LENGTH_ROWS), :] = zeros
            length_ref[half, pl.ds(k, HALF + 8, stride=LENGTH_ROWS), :] = jnp.zeros((HALF + 8, LANES), jnp.float32)
        for k in range(18, 21):
            inner_ref[half, pl.ds(k, HALF, stride=LENGTH_ROWS), :] = ones
            length_ref[half, pl.ds(k, HALF + 8, stride=LENGTH_ROWS), :] = jnp.ones((HALF + 8, LANES), jnp.float32)

    for group in range(groups):
        a = runs[group]
        b = []
        for q in range(3):
            end = jnp.where(
                last, runs[(group + 1) % groups][q][0:1, 0:1], pltpu.roll(a[q][0:1, :], LANES - 1, 1)
            )
            b.append(jnp.concatenate([a[q][1:], end], axis=0))
        g = strength[group * LANES : (group + 1) * LANES].T
        ends = [g * (a[q] - b[q]) for q in range(3)]
        ends += [
            g * (a[1] * b[2] - a[2] * b[1]),
            g * (a[2] * b[0] - a[0] * b[2]),
            g * (a[0] * b[1] - a[1] * b[0]),
        ]
        for k in range(6):
            pieces = three_pieces(ends[k])
            for p in range(6):
                put(normal_ref, NORMAL_ROWS, 0, p * 6 + k, pieces[PIECE_OF_SEGMENT[p]])
        for k in range(3):
            pieces = three_pieces(-(a[k] + b[k]))
            for p in range(6):
                put(inner_ref, LENGTH_ROWS, 0, p * 3 + k, pieces[PIECE_OF_SEGMENT[p]])
            pieces = three_pieces(-2.0 * b[k])
            first = three_pieces(-2.0 * a[k])
            for p in range(6):
                put(length_ref, LENGTH_ROWS, 1, p * 3 + k, pieces[PIECE_OF_SEGMENT[p]])
                for half in range(2):
                    length_ref[half, p * 3 + k : p * 3 + k + 1, :] = first[PIECE_OF_SEGMENT[p]][half * HALF : half * HALF + 1]
        pieces = three_pieces(a[0] * b[0] + a[1] * b[1] + a[2] * b[2])
        for k in range(3):
            put(inner_ref, LENGTH_ROWS, 0, 21 + k, pieces[k])
        pieces = three_pieces(b[0] * b[0] + b[1] * b[1] + b[2] * b[2])
        first = three_pieces(a[0] * a[0] + a[1] * a[1] + a[2] * a[2])
        for k in range(3):
            put(length_ref, LENGTH_ROWS, 1, 21 + k, pieces[k])
            for half in range(2):
                length_ref[half, 21 + k : 22 + k, :] = first[k][half * HALF : half * HALF + 1]

        def narrow(i, carry):
            for source, target, size in (
                (normal_ref, normal_bf_ref, NORMAL_ROWS),
                (length_ref, length_bf_ref, LENGTH_ROWS),
                (inner_ref, inner_bf_ref, LENGTH_ROWS),
            ):
                part = pl.ds(pl.multiple_of(i * size, size), size)
                for half in range(2):
                    target[part, half * LANES : (half + 1) * LANES] = source[half, part, :].astype(jnp.bfloat16)
            return carry

        lax.fori_loop(0, HALF, narrow, 0, unroll=8)
        part = pl.ds(HALF * LENGTH_ROWS, LENGTH_ROWS)
        for half in range(2):
            length_bf_ref[part, half * LANES : (half + 1) * LANES] = length_ref[half, part, :].astype(jnp.bfloat16)

        def panel_step(b, carry):
            part = pl.ds(pl.multiple_of(b * PANEL_STEP, PANEL_STEP), PANEL_STEP)
            normal_side = normal_side_ref[part, :]
            length_side = length_side_ref[part, :]

            def form(side, ref, size, i, k):
                weights = ref[pl.ds(pl.multiple_of(i * size, size) + k * size, size), :]
                return jnp.dot(side, weights, preferred_element_type=jnp.float32)

            def length_of(square):
                square = jnp.maximum(square, 1e-30)
                return square * lax.rsqrt(square)

            def node_step(block, state):
                length, total = state
                first = block * NODE_STEP
                for k in range(NODE_STEP):
                    normal_part = form(normal_side, normal_bf_ref, NORMAL_ROWS, first, k)
                    inner = form(length_side, inner_bf_ref, LENGTH_ROWS, first, k)
                    after = length_of(form(length_side, length_bf_ref, LENGTH_ROWS, first, k + 1))
                    product = length * after
                    below = product * (product + inner) + CORE_SQ
                    total = total + ((length + after) * normal_part) * pl.reciprocal(below)
                    length = after
                return length, total

            start = (
                length_of(form(length_side, length_bf_ref, LENGTH_ROWS, 0, 0)),
                jnp.zeros((PANEL_STEP, WIDE), jnp.float32),
            )
            _, total = lax.fori_loop(0, HALF // NODE_STEP, node_step, start)
            total_ref[part, :] += total[:, :LANES] + total[:, LANES:]
            return carry

        lax.fori_loop(0, piece_rows * LANES // PANEL_STEP, panel_step, 0)

    for r in range(piece_rows):
        induced = jnp.sum(total_ref[r * LANES : (r + 1) * LANES, :].T, axis=0, keepdims=True)
        right_ref[r : r + 1, :] = -(onset_ref[r : r + 1, :] + induced)
    right = right_ref[...]
    for k in range(copies_ref.shape[0]):
        copies_ref[k] = right


def induce(nodes, panels, copies):
    piece = panels[0].shape[0]
    piece_rows = piece // LANES
    pairs = piece * nodes.size // 5
    return pl.pallas_call(
        induce_kernel,
        out_shape=(
            jax.ShapeDtypeStruct((piece_rows, LANES), jnp.float32),
            jax.ShapeDtypeStruct((copies, piece_rows, LANES), jnp.float32),
        ),
        in_specs=[VMEM] * 5,
        out_specs=(VMEM, VMEM),
        scratch_shapes=[
            pltpu.VMEM((2, HALF * NORMAL_ROWS, LANES), jnp.float32),
            pltpu.VMEM((2, (HALF + 8) * LENGTH_ROWS, LANES), jnp.float32),
            pltpu.VMEM((2, HALF * LENGTH_ROWS, LANES), jnp.float32),
            pltpu.VMEM((HALF * NORMAL_ROWS, WIDE), jnp.bfloat16),
            pltpu.VMEM(((HALF + 1) * LENGTH_ROWS, WIDE), jnp.bfloat16),
            pltpu.VMEM((HALF * LENGTH_ROWS, WIDE), jnp.bfloat16),
            pltpu.VMEM((piece, LANES), jnp.float32),
        ],
        compiler_params=pltpu.CompilerParams(vmem_limit_bytes=24 * 2**20),
        cost_estimate=pl.CostEstimate(flops=30 * pairs, bytes_accessed=2**21, transcendentals=2 * pairs),
        name="induce",
    )(nodes, *panels)


def whole_sum(value):
    return jnp.sum(value, keepdims=True)


def orthogonalize(image_ref, known_refs, column_ref):
    image = image_ref[...].reshape(-1, LANES)
    known = [ref[...] for ref in known_refs]
    coeffs = [whole_sum(image * member) for member in known]
    for coeff, member in zip(coeffs, known):
        image = image - coeff * member
    norm = jnp.sqrt(whole_sum(image * image))
    for i, value in enumerate(coeffs + [norm]):
        column_ref[i : i + 1, :] = jnp.broadcast_to(value, (1, LANES))
    return image / norm


def deal_kernel(place_ref, index_ref, near_ref, left_ref, *out_refs):
    n_col = len(out_refs) + 1
    rank, width = left_ref.shape
    piece_rows = width // LANES // n_col
    lane = lax.broadcasted_iota(jnp.int32, (8, LANES), 1)
    for shift in range(1, n_col):
        out_ref = out_refs[shift - 1]
        first = lax.rem(place_ref[1] + shift, n_col) * piece_rows
        index = jnp.zeros((8, LANES), jnp.float32)
        for r in range(piece_rows):
            base = r * (LANES + rank)
            out_ref[base : base + LANES, :] = near_ref[first + r]
            columns = pl.ds(pl.multiple_of((first + r) * LANES, LANES), LANES)
            out_ref[base + LANES : base + LANES + rank, :] = left_ref[:, columns]
            index = jnp.where(lane == r, index_ref[first + r].astype(jnp.float32), index)
        out_ref[piece_rows * (LANES + rank) :, :] = index


def deal(place, index, near, left, n_col):
    rank, width = left.shape
    piece_rows = width // LANES // n_col
    shape = jax.ShapeDtypeStruct((piece_rows * (LANES + rank) + 8, LANES), jnp.float32)
    return pl.pallas_call(
        deal_kernel,
        out_shape=(shape,) * (n_col - 1),
        in_specs=[SMEM, SMEM, VMEM, VMEM],
        out_specs=(VMEM,) * (n_col - 1),
        compiler_params=pltpu.CompilerParams(vmem_limit_bytes=16 * 2**20),
        name="deal",
    )(place, index, near, left)


def step_kernel(known_count, n_col, *refs):
    place_ref, index_refs, refs = refs[0], refs[1 : 1 + n_col], refs[1 + n_col :]
    image_ref, known_refs, refs = refs[0], refs[1 : 1 + known_count], refs[1 + known_count :]
    self_ref, near_ref, left_ref, refs = refs[0], refs[1], refs[2], refs[3:]
    dealt_refs, right_refs = refs[: n_col - 1], refs[n_col - 1 : 2 * n_col - 1]
    vector_ref, column_ref, copies_ref = refs[2 * n_col - 1 :]
    piece_rows = self_ref.shape[0]
    piece = piece_rows * LANES
    rank = right_refs[0].shape[0]
    n_wake = right_refs[0].shape[1] // piece
    vector_ref[...] = orthogonalize(image_ref, known_refs, column_ref)
    place, mine = place_ref[0], place_ref[1]

    far = [jnp.zeros((rank, LANES), jnp.float32) for _ in range(piece_rows)]
    near = [jnp.zeros((LANES, LANES), jnp.float32) for _ in range(piece_rows)]
    for shift in range(n_col):
        group = lax.rem(mine - shift + n_col, n_col)

        def chunk(w, total):
            first = (w * n_col + group) * piece_rows
            for r in range(piece_rows):
                entries = vector_ref[pl.ds(first + r, 1), :]
                columns = pl.ds(pl.multiple_of(w * piece, LANES) + r * LANES, LANES)
                total = total + right_refs[shift][:, columns] * entries
            return total

        coeff = lax.fori_loop(0, n_wake, chunk, jnp.zeros((rank, LANES), jnp.float32), unroll=4)
        coeff = jnp.sum(coeff, axis=1, keepdims=True)
        for r in range(piece_rows):
            if shift == 0:
                row_block = mine * piece_rows + r
                block = index_refs[0][row_block]
                left = left_ref[:, pl.ds(pl.multiple_of(row_block * LANES, LANES), LANES)]
                matrix = near_ref[row_block]
            else:
                base = r * (LANES + rank)
                block = index_refs[shift][r]
                left = dealt_refs[shift - 1][base + LANES : base + LANES + rank, :]
                matrix = dealt_refs[shift - 1][base : base + LANES, :]
            where = (lax.div(block, piece_rows) * n_col + group) * piece_rows + lax.rem(block, piece_rows)
            far[r] = far[r] + left * coeff
            near[r] = near[r] + matrix * vector_ref[pl.ds(where, 1), :]
    image = jnp.concatenate(
        [
            jnp.sum(near[r].T, axis=0, keepdims=True) + jnp.sum(far[r], axis=0, keepdims=True)
            for r in range(piece_rows)
        ],
        axis=0,
    )
    own = vector_ref[pl.ds(pl.multiple_of(place * piece_rows, piece_rows), piece_rows), :]
    image = self_ref[...] * own + image
    for k in range(copies_ref.shape[0]):
        copies_ref[k] = image


def arnoldi_step(place, indices, image, known, self_term, near, left, dealt, rights):
    copies, piece_rows, _ = image.shape
    total_rows = copies * piece_rows
    operands = [image, *known, self_term, near, left, *dealt, *rights]
    return pl.pallas_call(
        functools.partial(step_kernel, len(known), len(rights)),
        out_shape=(
            jax.ShapeDtypeStruct((total_rows, LANES), jnp.float32),
            jax.ShapeDtypeStruct((8, LANES), jnp.float32),
            jax.ShapeDtypeStruct((copies, piece_rows, LANES), jnp.float32),
        ),
        in_specs=[SMEM] * (1 + len(indices)) + [VMEM] * len(operands),
        out_specs=(VMEM, VMEM, VMEM),
        compiler_params=pltpu.CompilerParams(vmem_limit_bytes=24 * 2**20),
        name="arnoldi_step",
    )(place, *indices, *operands)


def small_solve(gram_matrix, projected):
    size_now = len(projected)
    factor = [[None for inner_pos in range(size_now)] for outer_pos in range(size_now)]
    for outer_pos in range(size_now):
        for inner_pos in range(outer_pos + 1):
            partial_sum = gram_matrix[outer_pos][inner_pos]
            for middle in range(inner_pos):
                partial_sum = partial_sum - factor[outer_pos][middle] * factor[inner_pos][middle]
            if inner_pos == outer_pos:
                factor[outer_pos][inner_pos] = jnp.sqrt(partial_sum)
            else:
                factor[outer_pos][inner_pos] = partial_sum / factor[inner_pos][inner_pos]
    forward = []
    for outer_pos in range(size_now):
        partial_sum = projected[outer_pos]
        for middle in range(outer_pos):
            partial_sum = partial_sum - factor[outer_pos][middle] * forward[middle]
        forward.append(partial_sum / factor[outer_pos][outer_pos])
    backward = [None for outer_pos in range(size_now)]
    for outer_pos in reversed(range(size_now)):
        partial_sum = forward[outer_pos]
        for middle in range(outer_pos + 1, size_now):
            partial_sum = partial_sum - factor[middle][outer_pos] * backward[middle]
        backward[outer_pos] = partial_sum / factor[outer_pos][outer_pos]
    return backward


def finish_kernel(place_ref, image_ref, *refs):
    known_refs, column_refs, out_ref, last_ref = refs[:KRYLOV], refs[KRYLOV : 2 * KRYLOV], refs[-2], refs[-1]
    orthogonalize(image_ref, known_refs, last_ref)
    norm = column_refs[0][0:1, :]
    columns = []
    for column, ref in enumerate(list(column_refs[1:]) + [last_ref]):
        columns.append([ref[i : i + 1, :] for i in range(column + 2)])
    gram = [
        [sum(columns[i][k] * columns[j][k] for k in range(j + 2)) for j in range(i + 1)]
        for i in range(KRYLOV)
    ]
    combination = small_solve(gram, [norm * columns[j][0] for j in range(KRYLOV)])
    piece_rows = out_ref.shape[0]
    part = pl.ds(pl.multiple_of(place_ref[0] * piece_rows, piece_rows), piece_rows)
    strengths = combination[0] * known_refs[0][part, :]
    for position in range(1, KRYLOV):
        strengths = strengths + combination[position] * known_refs[position][part, :]
    out_ref[...] = strengths


def finish(place, image, known, columns):
    piece_rows = image.shape[1]
    return pl.pallas_call(
        finish_kernel,
        out_shape=jax.ShapeDtypeStruct((piece_rows, LANES), jnp.float32),
        in_specs=[SMEM] + [VMEM] * (1 + len(known) + len(columns)),
        out_specs=VMEM,
        scratch_shapes=[pltpu.VMEM((8, LANES), jnp.float32)],
        compiler_params=pltpu.CompilerParams(vmem_limit_bytes=16 * 2**20),
        name="finish",
    )(place, image, *known, *columns)


def body(
    points,
    normals,
    freestream,
    wake_nodes,
    circulation,
    filament,
    self_term,
    near_blocks,
    near_index,
    far_left,
    far_right,
):
    everyone = ("wake", "col")
    n_wake, n_col = lax.axis_size("wake"), lax.axis_size("col")
    copies = n_wake * n_col
    piece = points.shape[1]
    piece_rows = piece // LANES
    mine = lax.axis_index("col")
    place = jnp.stack([lax.axis_index("wake") * n_col + mine, mine])

    near, index, left, right = near_blocks[:, 0, 0], near_index[:, 0, 0], far_left[0], far_right[0]
    dealt, indices, rights = [], [index], [right]
    for shift, part in enumerate(deal(place, index, near, left, n_col), 1):
        pairs = [(source, (source + shift) % n_col) for source in range(n_col)]
        dealt.append(lax.ppermute(part, "col", pairs))
        indices.append(dealt[-1][-8, :piece_rows].astype(jnp.int32))
        rights.append(lax.ppermute(right, "col", pairs))

    packed = pack_nodes(wake_nodes, circulation, filament, n_wake)
    panels = prepare_panels(points, normals, freestream)
    nodes = lax.all_to_all(packed, "wake", 0, 0, tiled=True)
    right_side, image_copies = induce(nodes, panels, copies)
    own_self = self_term.reshape(piece_rows, LANES)
    known, columns = [], []
    for _ in range(KRYLOV):
        image = lax.all_to_all(image_copies, everyone, 0, 0, tiled=True)
        vector, column, image_copies = arnoldi_step(
            place, indices, image, known, own_self, near, left, dealt, rights
        )
        known.append(vector)
        columns.append(column)
    image = lax.all_to_all(image_copies, everyone, 0, 0, tiled=True)
    strengths = finish(place, image, known, columns)
    return right_side.reshape(piece), strengths.reshape(piece)


def solution(mesh):
    in_specs = (
        P(None, ("wake", "col")),
        P(None, ("wake", "col")),
        P(),
        P(None, "wake"),
        P("wake"),
        P("wake"),
        P(("wake", "col")),
        P("wake", "col", None, None, None),
        P("wake", "col", None),
        P("col", None, "wake"),
        P("wake", None, "col"),
    )
    out_specs = (P(("wake", "col")), P(("wake", "col")))
    return jax.shard_map(body, mesh=mesh, in_specs=in_specs, out_specs=out_specs, check_vma=False)
```

```python
import functools
import math

import jax
import jax.numpy as jnp
from jax import lax
from jax.experimental import pallas as pl
from jax.experimental.pallas import tpu as pltpu
from jax.sharding import PartitionSpec as P

KRYLOV = 6
CORE_SQ = 0.01
FOUR_PI = 4.0 * math.pi
LANES = 128
NORMAL_PRODUCTS = ((0, 0), (0, 1), (1, 0), (0, 2), (2, 0))
LENGTH_PRODUCTS = NORMAL_PRODUCTS + ((1, 1),)
FEATURES = 32
RUN = 4
DEPTH = FEATURES * RUN
WIDE = 2 * LANES
HALF = LANES // 2
BLOCKS = HALF // RUN
PANEL_STEP = 256
BLOCK_STEP = 8

VMEM = pl.BlockSpec(memory_space=pltpu.VMEM)
SMEM = pl.BlockSpec(memory_space=pltpu.SMEM)
HBM = pl.BlockSpec(memory_space=pltpu.HBM)


def pack_kernel(nodes_ref, circulation_ref, filament_ref, out_ref):
    copies, _, rows, _ = out_ref.shape
    own = [
        jnp.concatenate([nodes_ref[q : q + 1, r * LANES : (r + 1) * LANES] for r in range(rows)], axis=0)
        for q in range(3)
    ]
    own.append(circulation_ref[...])
    own.append(filament_ref[...].astype(jnp.float32) + 1.0)
    for q in range(5):
        for k in range(copies):
            out_ref[k, q] = own[q]


def pack_nodes(wake_nodes, circulation, filament, copies):
    rows = circulation.shape[0] // LANES
    return pl.pallas_call(
        pack_kernel,
        out_shape=jax.ShapeDtypeStruct((copies, 5, rows, LANES), jnp.float32),
        in_specs=[VMEM, VMEM, VMEM],
        out_specs=VMEM,
        name="pack_nodes",
    )(wake_nodes, circulation.reshape(rows, LANES), filament.reshape(rows, LANES))


def three_pieces(value):
    high = value.astype(jnp.bfloat16).astype(jnp.float32)
    rest = value - high
    middle = rest.astype(jnp.bfloat16).astype(jnp.float32)
    low = (rest - middle).astype(jnp.bfloat16).astype(jnp.float32)
    return high, middle, low


def panels_kernel(
    points_ref, normals_ref, stream_ref, normal_side_out, length_side_out, info_out,
    normal_side_ref, length_side_ref, info_ref, left,
):
    piece_rows = info_ref.shape[0] - 8

    def spread(ref, q):
        return jnp.concatenate(
            [ref[q : q + 1, r * LANES : (r + 1) * LANES] for r in range(piece_rows)], axis=0
        )

    points = [spread(points_ref, q) for q in range(3)]
    normals = [spread(normals_ref, q) for q in range(3)]
    middle = [0.5 * (jnp.max(p, keepdims=True) + jnp.min(p, keepdims=True)) for p in points]
    info_ref[...] = jnp.zeros_like(info_ref)
    info_ref[0:piece_rows, :] = (
        stream_ref[0] * normals[0] + stream_ref[1] * normals[1] + stream_ref[2] * normals[2]
    )
    for q in range(3):
        info_ref[piece_rows + q : piece_rows + q + 1, :] = jnp.broadcast_to(middle[q], (1, LANES))
    px, py, pz = [points[q] - middle[q] for q in range(3)]
    features = [
        normals[1] * pz - normals[2] * py,
        normals[2] * px - normals[0] * pz,
        normals[0] * py - normals[1] * px,
        normals[0], normals[1], normals[2],
    ]
    blank = jnp.zeros_like(px)
    pieces = [three_pieces(feature) for feature in features]
    side = [pieces[k][p] for p, _ in NORMAL_PRODUCTS for k in range(6)]
    side += [blank] * (FEATURES - len(side))
    pieces = [three_pieces(value) for value in (px, py, pz)]
    side += [pieces[k][p] for p, _ in LENGTH_PRODUCTS for k in range(3)]
    side += list(three_pieces(px * px + py * py + pz * pz)) + [jnp.ones_like(px)] * 3
    side += [blank] * (LANES - len(side))
    column = lax.broadcasted_iota(jnp.int32, (FEATURES, DEPTH), 1)
    first = lax.broadcasted_iota(jnp.int32, (FEATURES, DEPTH), 0) * RUN
    again = jnp.where((column >= first) & (column < first + RUN), 1.0, 0.0).astype(jnp.bfloat16)
    for r in range(piece_rows):
        own = slice(r * LANES, (r + 1) * LANES)
        turned = jnp.concatenate([value[r : r + 1, :] for value in side], axis=0).T.astype(jnp.bfloat16)
        for ref, start in ((normal_side_ref, 0), (length_side_ref, FEATURES)):
            wide = jnp.dot(turned[:, start : start + FEATURES], again, preferred_element_type=jnp.float32)
            ref[own, :] = wide.astype(jnp.bfloat16)
    leaving = [
        pltpu.make_async_copy(source, target, left.at[i])
        for i, (source, target) in enumerate(
            (
                (normal_side_ref, normal_side_out),
                (length_side_ref, length_side_out),
                (info_ref, info_out),
            )
        )
    ]
    for copy in leaving:
        copy.start()
    for copy in leaving:
        copy.wait()


def prepare_panels(points, normals, freestream):
    piece = points.shape[1]
    return pl.pallas_call(
        panels_kernel,
        out_shape=(
            jax.ShapeDtypeStruct((piece, DEPTH), jnp.bfloat16),
            jax.ShapeDtypeStruct((piece, DEPTH), jnp.bfloat16),
            jax.ShapeDtypeStruct((piece // LANES + 8, LANES), jnp.float32),
        ),
        in_specs=[VMEM, VMEM, SMEM],
        out_specs=(HBM, HBM, HBM),
        scratch_shapes=[
            pltpu.VMEM((piece, DEPTH), jnp.bfloat16),
            pltpu.VMEM((piece, DEPTH), jnp.bfloat16),
            pltpu.VMEM((piece // LANES + 8, LANES), jnp.float32),
            pltpu.SemaphoreType.DMA((3,)),
        ],
        name="prepare_panels",
    )(points, normals, freestream)


def induce_kernel(
    nodes_in, normal_side_in, length_side_in, info_in, right_ref, copies_ref,
    nodes_ref, normal_side_ref, length_side_ref, info_ref,
    normal_ref, length_ref, inner_ref, normal_pick_ref, length_pick_ref, total_ref, arrived,
):
    fetches = [
        pltpu.make_async_copy(source, target, arrived.at[i])
        for i, (source, target) in enumerate(
            (
                (nodes_in, nodes_ref),
                (info_in, info_ref),
                (normal_side_in, normal_side_ref),
                (length_side_in, length_side_ref),
            )
        )
    ]
    for fetch in fetches:
        fetch.start()
    fetches[0].wait()
    fetches[1].wait()
    rows = nodes_ref.shape[0] * nodes_ref.shape[2]
    groups = rows // LANES
    x, y, z, circulation, tag = [nodes_ref[:, q].reshape(rows, LANES) for q in range(5)]
    piece_rows = right_ref.shape[0]
    lane = lax.broadcasted_iota(jnp.int32, (rows, LANES), 1)
    row = lax.broadcasted_iota(jnp.int32, (rows, LANES), 0)
    turned = pltpu.roll(tag, LANES - 1, 1)
    next_tag = jnp.where(lane == LANES - 1, pltpu.roll(turned, rows - 1, 0), turned)
    linked = (tag == next_tag) & ((lane < LANES - 1) | (row < rows - 1))
    strength = jnp.where(linked, circulation * (1.0 / FOUR_PI), 0.0)
    runs = [
        [
            (value - info_ref[piece_rows + q : piece_rows + q + 1, :])[g * LANES : (g + 1) * LANES].T
            for q, value in enumerate((x, y, z))
        ]
        for g in range(groups)
    ]
    total_ref[...] = jnp.zeros_like(total_ref)
    last = lax.broadcasted_iota(jnp.int32, (1, LANES), 1) == LANES - 1
    blank = jnp.zeros((LANES, LANES), jnp.float32)
    ones = jnp.ones((LANES, LANES), jnp.float32)

    def put(ref, features, blocks, to=0):
        features = features + [blank] * (FEATURES - len(features))
        count = 16 // RUN
        for k in range(0, FEATURES, count):
            for half in range(2):
                for block in range(blocks):
                    start = half * HALF + block * RUN
                    rows = jnp.concatenate([value[start : start + RUN] for value in features[k : k + count]], axis=0)
                    ref[to + block, k * RUN : (k + count) * RUN, half * LANES : (half + 1) * LANES] = rows.astype(
                        jnp.bfloat16
                    )

    for group in range(groups):
        a = runs[group]
        b = []
        for q in range(3):
            end = jnp.where(
                last, runs[(group + 1) % groups][q][0:1, 0:1], pltpu.roll(a[q][0:1, :], LANES - 1, 1)
            )
            b.append(jnp.concatenate([a[q][1:], end], axis=0))
        g = strength[group * LANES : (group + 1) * LANES].T
        ends = [g * (a[q] - b[q]) for q in range(3)]
        ends += [
            g * (a[1] * b[2] - a[2] * b[1]),
            g * (a[2] * b[0] - a[0] * b[2]),
            g * (a[0] * b[1] - a[1] * b[0]),
        ]
        pieces = [three_pieces(value) for value in ends]
        put(normal_ref, [pieces[k][p] for _, p in NORMAL_PRODUCTS for k in range(6)], BLOCKS)

        def length_rows(linear, square):
            pieces = [three_pieces(value) for value in linear]
            rows = [pieces[k][p] for _, p in LENGTH_PRODUCTS for k in range(3)]
            return rows + [ones] * 3 + list(three_pieces(square))

        inner = length_rows([-(a[q] + b[q]) for q in range(3)], a[0] * b[0] + a[1] * b[1] + a[2] * b[2])
        put(inner_ref, inner, BLOCKS)
        after = length_rows([-2.0 * b[q] for q in range(3)], b[0] * b[0] + b[1] * b[1] + b[2] * b[2])
        put(length_ref, after, BLOCKS)
        start = length_rows([-2.0 * a[q] for q in range(3)], a[0] * a[0] + a[1] * a[1] + a[2] * a[2])
        put(length_ref, start, 1, BLOCKS)
        if group == 0:
            fetches[2].wait()
            fetches[3].wait()

        def panel_step(b, carry):
            part = pl.ds(pl.multiple_of(b * PANEL_STEP, PANEL_STEP), PANEL_STEP)
            place = lax.broadcasted_iota(jnp.int32, (1, DEPTH), 1) % RUN
            for j in range(RUN):
                mask = jnp.where(place == j, 1.0, 0.0).astype(jnp.bfloat16)
                normal_pick_ref[j] = normal_side_ref[part, :] * mask
                length_pick_ref[j] = length_side_ref[part, :] * mask

            def form(pick_ref, j, weights):
                return jnp.dot(pick_ref[j], weights, preferred_element_type=jnp.float32)

            def length_of(square):
                square = jnp.maximum(square, 1e-30)
                return square * lax.rsqrt(square)

            def node_step(step, state):
                length, total = state
                for i in range(BLOCK_STEP):
                    block = step * BLOCK_STEP + i
                    for j in range(RUN):
                        normal_part = form(normal_pick_ref, j, normal_ref[block])
                        inner = form(length_pick_ref, j, inner_ref[block])
                        after = length_of(form(length_pick_ref, j, length_ref[block]))
                        product = length * after
                        below = product * (product + inner) + CORE_SQ
                        total = total + ((length + after) * normal_part) * pl.reciprocal(below)
                        length = after
                return length, total

            start = (
                length_of(form(length_pick_ref, 0, length_ref[BLOCKS])),
                jnp.zeros((PANEL_STEP, WIDE), jnp.float32),
            )
            _, total = lax.fori_loop(0, BLOCKS // BLOCK_STEP, node_step, start)
            total_ref[part, :] += total[:, :LANES] + total[:, LANES:]
            return carry

        lax.fori_loop(0, piece_rows * LANES // PANEL_STEP, panel_step, 0)

    for r in range(piece_rows):
        induced = jnp.sum(total_ref[r * LANES : (r + 1) * LANES, :].T, axis=0, keepdims=True)
        right_ref[r : r + 1, :] = -(info_ref[r : r + 1, :] + induced)
    right = right_ref[...]
    for k in range(copies_ref.shape[0]):
        copies_ref[k] = right


def induce(nodes, panels, copies):
    piece = panels[0].shape[0]
    piece_rows = piece // LANES
    pairs = piece * nodes.size // 5
    return pl.pallas_call(
        induce_kernel,
        out_shape=(
            jax.ShapeDtypeStruct((piece_rows, LANES), jnp.float32),
            jax.ShapeDtypeStruct((copies, piece_rows, LANES), jnp.float32),
        ),
        in_specs=[HBM] * 4,
        out_specs=(VMEM, VMEM),
        scratch_shapes=[
            pltpu.VMEM(nodes.shape, jnp.float32),
            pltpu.VMEM((piece, DEPTH), jnp.bfloat16),
            pltpu.VMEM((piece, DEPTH), jnp.bfloat16),
            pltpu.VMEM((piece_rows + 8, LANES), jnp.float32),
            pltpu.VMEM((BLOCKS, DEPTH, WIDE), jnp.bfloat16),
            pltpu.VMEM((BLOCKS + 1, DEPTH, WIDE), jnp.bfloat16),
            pltpu.VMEM((BLOCKS, DEPTH, WIDE), jnp.bfloat16),
            pltpu.VMEM((RUN, PANEL_STEP, DEPTH), jnp.bfloat16),
            pltpu.VMEM((RUN, PANEL_STEP, DEPTH), jnp.bfloat16),
            pltpu.VMEM((piece, LANES), jnp.float32),
            pltpu.SemaphoreType.DMA((4,)),
        ],
        compiler_params=pltpu.CompilerParams(vmem_limit_bytes=60 * 2**20),
        cost_estimate=pl.CostEstimate(flops=30 * pairs, bytes_accessed=2**21, transcendentals=2 * pairs),
        name="induce",
    )(nodes, *panels)


def whole_sum(value):
    return jnp.sum(value, keepdims=True)


def orthogonalize(image_ref, known_refs, column_ref):
    image = image_ref[...].reshape(-1, LANES)
    known = [ref[...] for ref in known_refs]
    coeffs = [whole_sum(image * member) for member in known]
    for coeff, member in zip(coeffs, known):
        image = image - coeff * member
    norm = jnp.sqrt(whole_sum(image * image))
    for i, value in enumerate(coeffs + [norm]):
        column_ref[i : i + 1, :] = jnp.broadcast_to(value, (1, LANES))
    return image / norm


def deal_kernel(place_ref, index_ref, near_ref, left_ref, *out_refs):
    n_col = len(out_refs) + 1
    rank, width = left_ref.shape
    piece_rows = width // LANES // n_col
    lane = lax.broadcasted_iota(jnp.int32, (8, LANES), 1)
    for shift in range(1, n_col):
        out_ref = out_refs[shift - 1]
        first = lax.rem(place_ref[1] + shift, n_col) * piece_rows
        index = jnp.zeros((8, LANES), jnp.float32)
        for r in range(piece_rows):
            base = r * (LANES + rank)
            out_ref[base : base + LANES, :] = near_ref[first + r]
            columns = pl.ds(pl.multiple_of((first + r) * LANES, LANES), LANES)
            out_ref[base + LANES : base + LANES + rank, :] = left_ref[:, columns]
            index = jnp.where(lane == r, index_ref[first + r].astype(jnp.float32), index)
        out_ref[piece_rows * (LANES + rank) :, :] = index


def deal(place, index, near, left, n_col):
    rank, width = left.shape
    piece_rows = width // LANES // n_col
    shape = jax.ShapeDtypeStruct((piece_rows * (LANES + rank) + 8, LANES), jnp.float32)
    return pl.pallas_call(
        deal_kernel,
        out_shape=(shape,) * (n_col - 1),
        in_specs=[SMEM, SMEM, VMEM, VMEM],
        out_specs=(VMEM,) * (n_col - 1),
        compiler_params=pltpu.CompilerParams(vmem_limit_bytes=16 * 2**20),
        name="deal",
    )(place, index, near, left)


def step_kernel(known_count, n_col, opening, *refs):
    place_ref, own_index_ref, refs = refs[0], refs[1], refs[2:]
    other = n_col - 1
    index_refs, refs = (None, refs) if opening else (refs[:other], refs[other:])
    image_ref, known_refs, refs = refs[0], refs[1 : 1 + known_count], refs[1 + known_count :]
    self_ref, near_ref, left_ref, right_ref, refs = refs[0], refs[1], refs[2], refs[3], refs[4:]
    dealt_refs, right_refs, refs = refs[:other], refs[other : 2 * other], refs[2 * other :]
    vector_ref, column_ref, copies_ref = refs[:3]
    fetches = []
    if opening:
        dealt_in, right_in = dealt_refs, right_refs
        refs = refs[3:]
        index_refs, dealt_refs, right_refs = refs[:other], refs[other : 2 * other], refs[2 * other : 3 * other]
        arrived = refs[3 * other]
        for i, (source, target) in enumerate(
            list(zip(dealt_in, dealt_refs)) + list(zip(right_in, right_refs))
        ):
            fetches.append(pltpu.make_async_copy(source, target, arrived.at[i]))
            fetches[-1].start()
    piece_rows = self_ref.shape[0]
    piece = piece_rows * LANES
    rank = right_ref.shape[0]
    n_wake = right_ref.shape[1] // piece
    vector_ref[...] = orthogonalize(image_ref, known_refs, column_ref)
    place, mine = place_ref[0], place_ref[1]
    for fetch in fetches:
        fetch.wait()
    if opening:
        lane = lax.broadcasted_iota(jnp.int32, (1, LANES), 1)
        for index_ref, dealt_ref in zip(index_refs, dealt_refs):
            last = dealt_ref.shape[0] - 8
            row = dealt_ref[last : last + 1, :]
            for r in range(piece_rows):
                index_ref[r] = jnp.sum(jnp.where(lane == r, row, 0.0)).astype(jnp.int32)
    index_refs = (own_index_ref, *index_refs)
    right_refs = (right_ref, *right_refs)

    far = [jnp.zeros((rank, LANES), jnp.float32) for _ in range(piece_rows)]
    near = [jnp.zeros((LANES, LANES), jnp.float32) for _ in range(piece_rows)]
    for shift in range(n_col):
        group = lax.rem(mine - shift + n_col, n_col)

        def chunk(w, total):
            first = (w * n_col + group) * piece_rows
            for r in range(piece_rows):
                entries = vector_ref[pl.ds(first + r, 1), :]
                columns = pl.ds(pl.multiple_of(w * piece, LANES) + r * LANES, LANES)
                total = total + right_refs[shift][:, columns] * entries
            return total

        coeff = lax.fori_loop(0, n_wake, chunk, jnp.zeros((rank, LANES), jnp.float32), unroll=4)
        coeff = jnp.sum(coeff, axis=1, keepdims=True)
        for r in range(piece_rows):
            if shift == 0:
                row_block = mine * piece_rows + r
                block = index_refs[0][row_block]
                left = left_ref[:, pl.ds(pl.multiple_of(row_block * LANES, LANES), LANES)]
                matrix = near_ref[row_block]
            else:
                base = r * (LANES + rank)
                block = index_refs[shift][r]
                left = dealt_refs[shift - 1][base + LANES : base + LANES + rank, :]
                matrix = dealt_refs[shift - 1][base : base + LANES, :]
            where = (lax.div(block, piece_rows) * n_col + group) * piece_rows + lax.rem(block, piece_rows)
            far[r] = far[r] + left * coeff
            near[r] = near[r] + matrix * vector_ref[pl.ds(where, 1), :]
    image = jnp.concatenate(
        [
            jnp.sum(near[r].T, axis=0, keepdims=True) + jnp.sum(far[r], axis=0, keepdims=True)
            for r in range(piece_rows)
        ],
        axis=0,
    )
    own = vector_ref[pl.ds(pl.multiple_of(place * piece_rows, piece_rows), piece_rows), :]
    image = self_ref[...] * own + image
    for k in range(copies_ref.shape[0]):
        copies_ref[k] = image


def arnoldi_step(place, index, image, known, self_term, near, left, right, others):
    copies, piece_rows, _ = image.shape
    opening = len(known) == 0
    dealt, rights = others[-2:]
    out_shape = [
        jax.ShapeDtypeStruct((copies * piece_rows, LANES), jnp.float32),
        jax.ShapeDtypeStruct((8, LANES), jnp.float32),
        jax.ShapeDtypeStruct((copies, piece_rows, LANES), jnp.float32),
    ]
    out_specs, scratch = [VMEM] * 3, []
    indices = [] if opening else others[0]
    operands = [image, *known, self_term, near, left, right]
    in_specs = [SMEM] * (2 + len(indices)) + [VMEM] * len(operands)
    in_specs += [HBM if opening else VMEM] * (len(dealt) + len(rights))
    if opening:
        out_shape += [jax.ShapeDtypeStruct((piece_rows,), jnp.int32) for _ in dealt]
        out_shape += [jax.ShapeDtypeStruct(value.shape, jnp.float32) for value in (*dealt, *rights)]
        out_specs += [SMEM] * len(dealt) + [VMEM] * (len(dealt) + len(rights))
        scratch = [pltpu.SemaphoreType.DMA((max(1, len(dealt) + len(rights)),))]
    results = pl.pallas_call(
        functools.partial(step_kernel, len(known), 1 + len(dealt), opening),
        out_shape=tuple(out_shape),
        in_specs=in_specs,
        out_specs=tuple(out_specs),
        scratch_shapes=scratch,
        compiler_params=pltpu.CompilerParams(vmem_limit_bytes=24 * 2**20),
        name="arnoldi_step",
    )(place, index, *indices, *operands, *dealt, *rights)
    if opening:
        count = len(dealt)
        rest = results[3:]
        others = (rest[:count], rest[count : 2 * count], rest[2 * count :])
    return results[:3], others


def small_solve(gram_matrix, projected):
    size_now = len(projected)
    factor = [[None for inner_pos in range(size_now)] for outer_pos in range(size_now)]
    for outer_pos in range(size_now):
        for inner_pos in range(outer_pos + 1):
            partial_sum = gram_matrix[outer_pos][inner_pos]
            for middle in range(inner_pos):
                partial_sum = partial_sum - factor[outer_pos][middle] * factor[inner_pos][middle]
            if inner_pos == outer_pos:
                factor[outer_pos][inner_pos] = jnp.sqrt(partial_sum)
            else:
                factor[outer_pos][inner_pos] = partial_sum / factor[inner_pos][inner_pos]
    forward = []
    for outer_pos in range(size_now):
        partial_sum = projected[outer_pos]
        for middle in range(outer_pos):
            partial_sum = partial_sum - factor[outer_pos][middle] * forward[middle]
        forward.append(partial_sum / factor[outer_pos][outer_pos])
    backward = [None for outer_pos in range(size_now)]
    for outer_pos in reversed(range(size_now)):
        partial_sum = forward[outer_pos]
        for middle in range(outer_pos + 1, size_now):
            partial_sum = partial_sum - factor[middle][outer_pos] * backward[middle]
        backward[outer_pos] = partial_sum / factor[outer_pos][outer_pos]
    return backward


def finish_kernel(place_ref, image_ref, *refs):
    known_refs, column_refs, out_ref, last_ref = refs[:KRYLOV], refs[KRYLOV : 2 * KRYLOV], refs[-2], refs[-1]
    orthogonalize(image_ref, known_refs, last_ref)
    norm = column_refs[0][0:1, :]
    columns = []
    for column, ref in enumerate(list(column_refs[1:]) + [last_ref]):
        columns.append([ref[i : i + 1, :] for i in range(column + 2)])
    gram = [
        [sum(columns[i][k] * columns[j][k] for k in range(j + 2)) for j in range(i + 1)]
        for i in range(KRYLOV)
    ]
    combination = small_solve(gram, [norm * columns[j][0] for j in range(KRYLOV)])
    piece_rows = out_ref.shape[0]
    part = pl.ds(pl.multiple_of(place_ref[0] * piece_rows, piece_rows), piece_rows)
    strengths = combination[0] * known_refs[0][part, :]
    for position in range(1, KRYLOV):
        strengths = strengths + combination[position] * known_refs[position][part, :]
    out_ref[...] = strengths


def finish(place, image, known, columns):
    piece_rows = image.shape[1]
    return pl.pallas_call(
        finish_kernel,
        out_shape=jax.ShapeDtypeStruct((piece_rows, LANES), jnp.float32),
        in_specs=[SMEM] + [VMEM] * (1 + len(known) + len(columns)),
        out_specs=VMEM,
        scratch_shapes=[pltpu.VMEM((8, LANES), jnp.float32)],
        compiler_params=pltpu.CompilerParams(vmem_limit_bytes=16 * 2**20),
        name="finish",
    )(place, image, *known, *columns)


def body(
    points,
    normals,
    freestream,
    wake_nodes,
    circulation,
    filament,
    self_term,
    near_blocks,
    near_index,
    far_left,
    far_right,
):
    everyone = ("wake", "col")
    n_wake, n_col = lax.axis_size("wake"), lax.axis_size("col")
    copies = n_wake * n_col
    piece = points.shape[1]
    piece_rows = piece // LANES
    mine = lax.axis_index("col")
    place = jnp.stack([lax.axis_index("wake") * n_col + mine, mine])

    near, index, left, right = near_blocks[:, 0, 0], near_index[:, 0, 0], far_left[0], far_right[0]
    dealt, rights = [], []
    for shift, part in enumerate(deal(place, index, near, left, n_col), 1):
        pairs = [(source, (source + shift) % n_col) for source in range(n_col)]
        dealt.append(lax.ppermute(part, "col", pairs))
        rights.append(lax.ppermute(right, "col", pairs))
    others = (dealt, rights)

    packed = pack_nodes(wake_nodes, circulation, filament, n_wake)
    panels = prepare_panels(points, normals, freestream)
    nodes = lax.all_to_all(packed, "wake", 0, 0, tiled=True)
    right_side, image_copies = induce(nodes, panels, copies)
    own_self = self_term.reshape(piece_rows, LANES)
    known, columns = [], []
    for _ in range(KRYLOV):
        image = lax.all_to_all(image_copies, everyone, 0, 0, tiled=True)
        (vector, column, image_copies), others = arnoldi_step(
            place, index, image, known, own_self, near, left, right, others
        )
        known.append(vector)
        columns.append(column)
    image = lax.all_to_all(image_copies, everyone, 0, 0, tiled=True)
    strengths = finish(place, image, known, columns)
    return right_side.reshape(piece), strengths.reshape(piece)


def solution(mesh):
    in_specs = (
        P(None, ("wake", "col")),
        P(None, ("wake", "col")),
        P(),
        P(None, "wake"),
        P("wake"),
        P("wake"),
        P(("wake", "col")),
        P("wake", "col", None, None, None),
        P("wake", "col", None),
        P("col", None, "wake"),
        P("wake", None, "col"),
    )
    out_specs = (P(("wake", "col")), P(("wake", "col")))
    return jax.shard_map(body, mesh=mesh, in_specs=in_specs, out_specs=out_specs, check_vma=False)
```

```python
import functools
import math

import jax
import jax.numpy as jnp
from jax import lax
from jax.experimental import pallas as pl
from jax.experimental.pallas import tpu as pltpu
from jax.sharding import PartitionSpec as P

KRYLOV = 6
CORE_SQ = 0.01
FOUR_PI = 4.0 * math.pi
LANES = 128
NORMAL_PRODUCTS = ((0, 0), (0, 1), (1, 0), (0, 2), (2, 0))
LENGTH_PRODUCTS = NORMAL_PRODUCTS + ((1, 1),)
FEATURES = 32
RUN = 4
DEPTH = FEATURES * RUN
WIDE = 2 * LANES
HALF = LANES // 2
BLOCKS = HALF // RUN
PANEL_STEP = 128
BLOCK_STEP = 16

VMEM = pl.BlockSpec(memory_space=pltpu.VMEM)
SMEM = pl.BlockSpec(memory_space=pltpu.SMEM)
HBM = pl.BlockSpec(memory_space=pltpu.HBM)


def pack_kernel(nodes_ref, circulation_ref, filament_ref, out_ref):
    copies, _, rows, _ = out_ref.shape
    own = [
        jnp.concatenate([nodes_ref[q : q + 1, r * LANES : (r + 1) * LANES] for r in range(rows)], axis=0)
        for q in range(3)
    ]
    own.append(circulation_ref[...])
    own.append(filament_ref[...].astype(jnp.float32) + 1.0)
    for q in range(5):
        for k in range(copies):
            out_ref[k, q] = own[q]


def pack_nodes(wake_nodes, circulation, filament, copies):
    rows = circulation.shape[0] // LANES
    return pl.pallas_call(
        pack_kernel,
        out_shape=jax.ShapeDtypeStruct((copies, 5, rows, LANES), jnp.float32),
        in_specs=[VMEM, VMEM, VMEM],
        out_specs=VMEM,
        name="pack_nodes",
    )(wake_nodes, circulation.reshape(rows, LANES), filament.reshape(rows, LANES))


def three_pieces(value):
    high = value.astype(jnp.bfloat16).astype(jnp.float32)
    rest = value - high
    middle = rest.astype(jnp.bfloat16).astype(jnp.float32)
    low = (rest - middle).astype(jnp.bfloat16).astype(jnp.float32)
    return high, middle, low


def panels_kernel(
    points_ref, normals_ref, stream_ref, normal_side_out, length_side_out, info_out,
    normal_side_ref, length_side_ref, info_ref, left,
):
    piece_rows = info_ref.shape[0] - 8

    def spread(ref, q):
        return jnp.concatenate(
            [ref[q : q + 1, r * LANES : (r + 1) * LANES] for r in range(piece_rows)], axis=0
        )

    points = [spread(points_ref, q) for q in range(3)]
    normals = [spread(normals_ref, q) for q in range(3)]
    middle = [0.5 * (jnp.max(p, keepdims=True) + jnp.min(p, keepdims=True)) for p in points]
    info_ref[...] = jnp.zeros_like(info_ref)
    info_ref[0:piece_rows, :] = (
        stream_ref[0] * normals[0] + stream_ref[1] * normals[1] + stream_ref[2] * normals[2]
    )
    for q in range(3):
        info_ref[piece_rows + q : piece_rows + q + 1, :] = jnp.broadcast_to(middle[q], (1, LANES))
    px, py, pz = [points[q] - middle[q] for q in range(3)]
    features = [
        normals[1] * pz - normals[2] * py,
        normals[2] * px - normals[0] * pz,
        normals[0] * py - normals[1] * px,
        normals[0], normals[1], normals[2],
    ]
    blank = jnp.zeros_like(px)
    pieces = [three_pieces(feature) for feature in features]
    side = [pieces[k][p] for p, _ in NORMAL_PRODUCTS for k in range(6)]
    side += [blank] * (FEATURES - len(side))
    pieces = [three_pieces(value) for value in (px, py, pz)]
    side += [pieces[k][p] for p, _ in LENGTH_PRODUCTS for k in range(3)]
    side += list(three_pieces(px * px + py * py + pz * pz)) + [jnp.ones_like(px)] * 3
    side += [blank] * (LANES - len(side))
    column = lax.broadcasted_iota(jnp.int32, (FEATURES, DEPTH), 1)
    first = lax.broadcasted_iota(jnp.int32, (FEATURES, DEPTH), 0) * RUN
    again = jnp.where((column >= first) & (column < first + RUN), 1.0, 0.0).astype(jnp.bfloat16)
    for r in range(piece_rows):
        own = slice(r * LANES, (r + 1) * LANES)
        turned = jnp.concatenate([value[r : r + 1, :] for value in side], axis=0).T.astype(jnp.bfloat16)
        for ref, start in ((normal_side_ref, 0), (length_side_ref, FEATURES)):
            wide = jnp.dot(turned[:, start : start + FEATURES], again, preferred_element_type=jnp.float32)
            ref[own, :] = wide.astype(jnp.bfloat16)
    leaving = [
        pltpu.make_async_copy(source, target, left.at[i])
        for i, (source, target) in enumerate(
            (
                (normal_side_ref, normal_side_out),
                (length_side_ref, length_side_out),
                (info_ref, info_out),
            )
        )
    ]
    for copy in leaving:
        copy.start()
    for copy in leaving:
        copy.wait()


def prepare_panels(points, normals, freestream):
    piece = points.shape[1]
    return pl.pallas_call(
        panels_kernel,
        out_shape=(
            jax.ShapeDtypeStruct((piece, DEPTH), jnp.bfloat16),
            jax.ShapeDtypeStruct((piece, DEPTH), jnp.bfloat16),
            jax.ShapeDtypeStruct((piece // LANES + 8, LANES), jnp.float32),
        ),
        in_specs=[VMEM, VMEM, SMEM],
        out_specs=(HBM, HBM, HBM),
        scratch_shapes=[
            pltpu.VMEM((piece, DEPTH), jnp.bfloat16),
            pltpu.VMEM((piece, DEPTH), jnp.bfloat16),
            pltpu.VMEM((piece // LANES + 8, LANES), jnp.float32),
            pltpu.SemaphoreType.DMA((3,)),
        ],
        name="prepare_panels",
    )(points, normals, freestream)


def induce_kernel(
    nodes_in, normal_side_in, length_side_in, info_in, right_ref, copies_ref,
    nodes_ref, normal_side_ref, length_side_ref, info_ref,
    normal_ref, length_ref, square_ref, normal_pick_ref, length_pick_ref, total_ref, arrived,
):
    fetches = [
        pltpu.make_async_copy(source, target, arrived.at[i])
        for i, (source, target) in enumerate(
            (
                (nodes_in, nodes_ref),
                (info_in, info_ref),
                (normal_side_in, normal_side_ref),
                (length_side_in, length_side_ref),
            )
        )
    ]
    for fetch in fetches:
        fetch.start()
    fetches[0].wait()
    fetches[1].wait()
    rows = nodes_ref.shape[0] * nodes_ref.shape[2]
    groups = rows // LANES
    x, y, z, circulation, tag = [nodes_ref[:, q].reshape(rows, LANES) for q in range(5)]
    piece_rows = right_ref.shape[0]
    lane = lax.broadcasted_iota(jnp.int32, (rows, LANES), 1)
    row = lax.broadcasted_iota(jnp.int32, (rows, LANES), 0)
    turned = pltpu.roll(tag, LANES - 1, 1)
    next_tag = jnp.where(lane == LANES - 1, pltpu.roll(turned, rows - 1, 0), turned)
    linked = (tag == next_tag) & ((lane < LANES - 1) | (row < rows - 1))
    strength = jnp.where(linked, circulation * (2.0 / FOUR_PI), 0.0)
    runs = [
        [
            (value - info_ref[piece_rows + q : piece_rows + q + 1, :])[g * LANES : (g + 1) * LANES].T
            for q, value in enumerate((x, y, z))
        ]
        for g in range(groups)
    ]
    total_ref[...] = jnp.zeros_like(total_ref)
    last = lax.broadcasted_iota(jnp.int32, (1, LANES), 1) == LANES - 1
    blank = jnp.zeros((LANES, LANES), jnp.float32)
    ones = jnp.ones((LANES, LANES), jnp.float32)

    def put(ref, features, blocks, to=0):
        features = features + [blank] * (FEATURES - len(features))
        count = 16 // RUN
        for k in range(0, FEATURES, count):
            for half in range(2):
                for block in range(blocks):
                    start = half * HALF + block * RUN
                    rows = jnp.concatenate([value[start : start + RUN] for value in features[k : k + count]], axis=0)
                    ref[to + block, k * RUN : (k + count) * RUN, half * LANES : (half + 1) * LANES] = rows.astype(
                        jnp.bfloat16
                    )

    for group in range(groups):
        a = runs[group]
        b = []
        for q in range(3):
            end = jnp.where(
                last, runs[(group + 1) % groups][q][0:1, 0:1], pltpu.roll(a[q][0:1, :], LANES - 1, 1)
            )
            b.append(jnp.concatenate([a[q][1:], end], axis=0))
        g = strength[group * LANES : (group + 1) * LANES].T
        ends = [g * (a[q] - b[q]) for q in range(3)]
        ends += [
            g * (a[1] * b[2] - a[2] * b[1]),
            g * (a[2] * b[0] - a[0] * b[2]),
            g * (a[0] * b[1] - a[1] * b[0]),
        ]
        pieces = [three_pieces(value) for value in ends]
        put(normal_ref, [pieces[k][p] for _, p in NORMAL_PRODUCTS for k in range(6)], BLOCKS)

        def length_rows(linear, square):
            pieces = [three_pieces(value) for value in linear]
            rows = [pieces[k][p] for _, p in LENGTH_PRODUCTS for k in range(3)]
            return rows + [ones] * 3 + list(three_pieces(square))

        square = sum((a[q] - b[q]) * (a[q] - b[q]) for q in range(3))
        for half in range(2):
            square_ref[:, half * LANES : (half + 1) * LANES] = square[half * HALF : (half + 1) * HALF]
        after = length_rows([-2.0 * b[q] for q in range(3)], b[0] * b[0] + b[1] * b[1] + b[2] * b[2])
        put(length_ref, after, BLOCKS)
        start = length_rows([-2.0 * a[q] for q in range(3)], a[0] * a[0] + a[1] * a[1] + a[2] * a[2])
        put(length_ref, start, 1, BLOCKS)
        if group == 0:
            fetches[2].wait()
            fetches[3].wait()

        def panel_step(b, carry):
            part = pl.ds(pl.multiple_of(b * PANEL_STEP, PANEL_STEP), PANEL_STEP)
            place = lax.broadcasted_iota(jnp.int32, (1, DEPTH), 1) % RUN
            for j in range(RUN):
                mask = jnp.where(place == j, 1.0, 0.0).astype(jnp.bfloat16)
                normal_pick_ref[j] = normal_side_ref[part, :] * mask
                length_pick_ref[j] = length_side_ref[part, :] * mask

            def form(pick_ref, j, weights):
                return jnp.dot(pick_ref[j], weights, preferred_element_type=jnp.float32)

            def length_of(square):
                square = jnp.maximum(square, 1e-30)
                return square * lax.rsqrt(square)

            def node_step(step, state):
                length, total = state
                for i in range(BLOCK_STEP):
                    block = step * BLOCK_STEP + i
                    for j in range(RUN):
                        normal_part = form(normal_pick_ref, j, normal_ref[block])
                        after = length_of(form(length_pick_ref, j, length_ref[block]))
                        reach = length + after
                        gap = reach * reach - square_ref[pl.ds(block * RUN + j, 1), :]
                        below = (length * after) * gap + 2.0 * CORE_SQ
                        total = total + (reach * normal_part) * pl.reciprocal(below)
                        length = after
                return length, total

            start = (
                length_of(form(length_pick_ref, 0, length_ref[BLOCKS])),
                jnp.zeros((PANEL_STEP, WIDE), jnp.float32),
            )
            _, total = lax.fori_loop(0, BLOCKS // BLOCK_STEP, node_step, start)
            total_ref[part, :] += total[:, :LANES] + total[:, LANES:]
            return carry

        lax.fori_loop(0, piece_rows * LANES // PANEL_STEP, panel_step, 0)

    for r in range(piece_rows):
        induced = jnp.sum(total_ref[r * LANES : (r + 1) * LANES, :].T, axis=0, keepdims=True)
        right_ref[r : r + 1, :] = -(info_ref[r : r + 1, :] + induced)
    right = right_ref[...]
    for k in range(copies_ref.shape[0]):
        copies_ref[k] = right


def induce(nodes, panels, copies):
    piece = panels[0].shape[0]
    piece_rows = piece // LANES
    pairs = piece * nodes.size // 5
    return pl.pallas_call(
        induce_kernel,
        out_shape=(
            jax.ShapeDtypeStruct((piece_rows, LANES), jnp.float32),
            jax.ShapeDtypeStruct((copies, piece_rows, LANES), jnp.float32),
        ),
        in_specs=[HBM] * 4,
        out_specs=(VMEM, VMEM),
        scratch_shapes=[
            pltpu.VMEM(nodes.shape, jnp.float32),
            pltpu.VMEM((piece, DEPTH), jnp.bfloat16),
            pltpu.VMEM((piece, DEPTH), jnp.bfloat16),
            pltpu.VMEM((piece_rows + 8, LANES), jnp.float32),
            pltpu.VMEM((BLOCKS, DEPTH, WIDE), jnp.bfloat16),
            pltpu.VMEM((BLOCKS + 1, DEPTH, WIDE), jnp.bfloat16),
            pltpu.VMEM((HALF, WIDE), jnp.float32),
            pltpu.VMEM((RUN, PANEL_STEP, DEPTH), jnp.bfloat16),
            pltpu.VMEM((RUN, PANEL_STEP, DEPTH), jnp.bfloat16),
            pltpu.VMEM((piece, LANES), jnp.float32),
            pltpu.SemaphoreType.DMA((4,)),
        ],
        compiler_params=pltpu.CompilerParams(vmem_limit_bytes=60 * 2**20),
        cost_estimate=pl.CostEstimate(flops=30 * pairs, bytes_accessed=2**21, transcendentals=2 * pairs),
        name="induce",
    )(nodes, *panels)


def whole_sum(value):
    return jnp.sum(value, keepdims=True)


def orthogonalize(image_ref, known_refs, column_ref):
    image = image_ref[...].reshape(-1, LANES)
    known = [ref[...] for ref in known_refs]
    coeffs = [whole_sum(image * member) for member in known]
    for coeff, member in zip(coeffs, known):
        image = image - coeff * member
    norm = jnp.sqrt(whole_sum(image * image))
    for i, value in enumerate(coeffs + [norm]):
        column_ref[i : i + 1, :] = jnp.broadcast_to(value, (1, LANES))
    return image / norm


def deal_kernel(place_ref, index_ref, near_ref, left_ref, *out_refs):
    n_col = len(out_refs) + 1
    rank, width = left_ref.shape
    piece_rows = width // LANES // n_col
    lane = lax.broadcasted_iota(jnp.int32, (8, LANES), 1)
    for shift in range(1, n_col):
        out_ref = out_refs[shift - 1]
        first = lax.rem(place_ref[1] + shift, n_col) * piece_rows
        index = jnp.zeros((8, LANES), jnp.float32)
        for r in range(piece_rows):
            base = r * (LANES + rank)
            out_ref[base : base + LANES, :] = near_ref[first + r]
            columns = pl.ds(pl.multiple_of((first + r) * LANES, LANES), LANES)
            out_ref[base + LANES : base + LANES + rank, :] = left_ref[:, columns]
            index = jnp.where(lane == r, index_ref[first + r].astype(jnp.float32), index)
        out_ref[piece_rows * (LANES + rank) :, :] = index


def deal(place, index, near, left, n_col):
    rank, width = left.shape
    piece_rows = width // LANES // n_col
    shape = jax.ShapeDtypeStruct((piece_rows * (LANES + rank) + 8, LANES), jnp.float32)
    return pl.pallas_call(
        deal_kernel,
        out_shape=(shape,) * (n_col - 1),
        in_specs=[SMEM, SMEM, VMEM, VMEM],
        out_specs=(VMEM,) * (n_col - 1),
        compiler_params=pltpu.CompilerParams(vmem_limit_bytes=16 * 2**20),
        name="deal",
    )(place, index, near, left)


def step_kernel(known_count, n_col, opening, *refs):
    place_ref, own_index_ref, refs = refs[0], refs[1], refs[2:]
    other = n_col - 1
    index_refs, refs = (None, refs) if opening else (refs[:other], refs[other:])
    image_ref, known_refs, refs = refs[0], refs[1 : 1 + known_count], refs[1 + known_count :]
    self_ref, near_ref, left_ref, right_ref, refs = refs[0], refs[1], refs[2], refs[3], refs[4:]
    dealt_refs, right_refs, refs = refs[:other], refs[other : 2 * other], refs[2 * other :]
    vector_ref, column_ref, copies_ref = refs[:3]
    fetches = []
    if opening:
        dealt_in, right_in = dealt_refs, right_refs
        refs = refs[3:]
        index_refs, dealt_refs, right_refs = refs[:other], refs[other : 2 * other], refs[2 * other : 3 * other]
        arrived = refs[3 * other]
        for i, (source, target) in enumerate(
            list(zip(dealt_in, dealt_refs)) + list(zip(right_in, right_refs))
        ):
            fetches.append(pltpu.make_async_copy(source, target, arrived.at[i]))
            fetches[-1].start()
    piece_rows = self_ref.shape[0]
    piece = piece_rows * LANES
    rank = right_ref.shape[0]
    n_wake = right_ref.shape[1] // piece
    vector_ref[...] = orthogonalize(image_ref, known_refs, column_ref)
    place, mine = place_ref[0], place_ref[1]
    for fetch in fetches:
        fetch.wait()
    if opening:
        lane = lax.broadcasted_iota(jnp.int32, (1, LANES), 1)
        for index_ref, dealt_ref in zip(index_refs, dealt_refs):
            last = dealt_ref.shape[0] - 8
            row = dealt_ref[last : last + 1, :]
            for r in range(piece_rows):
                index_ref[r] = jnp.sum(jnp.where(lane == r, row, 0.0)).astype(jnp.int32)
    index_refs = (own_index_ref, *index_refs)
    right_refs = (right_ref, *right_refs)

    far = [jnp.zeros((rank, LANES), jnp.float32) for _ in range(piece_rows)]
    near = [jnp.zeros((LANES, LANES), jnp.float32) for _ in range(piece_rows)]
    for shift in range(n_col):
        group = lax.rem(mine - shift + n_col, n_col)

        def chunk(w, total):
            first = (w * n_col + group) * piece_rows
            for r in range(piece_rows):
                entries = vector_ref[pl.ds(first + r, 1), :]
                columns = pl.ds(pl.multiple_of(w * piece, LANES) + r * LANES, LANES)
                total = total + right_refs[shift][:, columns] * entries
            return total

        coeff = lax.fori_loop(0, n_wake, chunk, jnp.zeros((rank, LANES), jnp.float32), unroll=4)
        coeff = jnp.sum(coeff, axis=1, keepdims=True)
        for r in range(piece_rows):
            if shift == 0:
                row_block = mine * piece_rows + r
                block = index_refs[0][row_block]
                left = left_ref[:, pl.ds(pl.multiple_of(row_block * LANES, LANES), LANES)]
                matrix = near_ref[row_block]
            else:
                base = r * (LANES + rank)
                block = index_refs[shift][r]
                left = dealt_refs[shift - 1][base + LANES : base + LANES + rank, :]
                matrix = dealt_refs[shift - 1][base : base + LANES, :]
            where = (lax.div(block, piece_rows) * n_col + group) * piece_rows + lax.rem(block, piece_rows)
            far[r] = far[r] + left * coeff
            near[r] = near[r] + matrix * vector_ref[pl.ds(where, 1), :]
    image = jnp.concatenate(
        [
            jnp.sum(near[r].T, axis=0, keepdims=True) + jnp.sum(far[r], axis=0, keepdims=True)
            for r in range(piece_rows)
        ],
        axis=0,
    )
    own = vector_ref[pl.ds(pl.multiple_of(place * piece_rows, piece_rows), piece_rows), :]
    image = self_ref[...] * own + image
    for k in range(copies_ref.shape[0]):
        copies_ref[k] = image


def arnoldi_step(place, index, image, known, self_term, near, left, right, others):
    copies, piece_rows, _ = image.shape
    opening = len(known) == 0
    dealt, rights = others[-2:]
    out_shape = [
        jax.ShapeDtypeStruct((copies * piece_rows, LANES), jnp.float32),
        jax.ShapeDtypeStruct((8, LANES), jnp.float32),
        jax.ShapeDtypeStruct((copies, piece_rows, LANES), jnp.float32),
    ]
    out_specs, scratch = [VMEM] * 3, []
    indices = [] if opening else others[0]
    operands = [image, *known, self_term, near, left, right]
    in_specs = [SMEM] * (2 + len(indices)) + [VMEM] * len(operands)
    in_specs += [HBM if opening else VMEM] * (len(dealt) + len(rights))
    if opening:
        out_shape += [jax.ShapeDtypeStruct((piece_rows,), jnp.int32) for _ in dealt]
        out_shape += [jax.ShapeDtypeStruct(value.shape, jnp.float32) for value in (*dealt, *rights)]
        out_specs += [SMEM] * len(dealt) + [VMEM] * (len(dealt) + len(rights))
        scratch = [pltpu.SemaphoreType.DMA((max(1, len(dealt) + len(rights)),))]
    results = pl.pallas_call(
        functools.partial(step_kernel, len(known), 1 + len(dealt), opening),
        out_shape=tuple(out_shape),
        in_specs=in_specs,
        out_specs=tuple(out_specs),
        scratch_shapes=scratch,
        compiler_params=pltpu.CompilerParams(vmem_limit_bytes=24 * 2**20),
        name="arnoldi_step",
    )(place, index, *indices, *operands, *dealt, *rights)
    if opening:
        count = len(dealt)
        rest = results[3:]
        others = (rest[:count], rest[count : 2 * count], rest[2 * count :])
    return results[:3], others


def small_solve(gram_matrix, projected):
    size_now = len(projected)
    factor = [[None for inner_pos in range(size_now)] for outer_pos in range(size_now)]
    for outer_pos in range(size_now):
        for inner_pos in range(outer_pos + 1):
            partial_sum = gram_matrix[outer_pos][inner_pos]
            for middle in range(inner_pos):
                partial_sum = partial_sum - factor[outer_pos][middle] * factor[inner_pos][middle]
            if inner_pos == outer_pos:
                factor[outer_pos][inner_pos] = jnp.sqrt(partial_sum)
            else:
                factor[outer_pos][inner_pos] = partial_sum / factor[inner_pos][inner_pos]
    forward = []
    for outer_pos in range(size_now):
        partial_sum = projected[outer_pos]
        for middle in range(outer_pos):
            partial_sum = partial_sum - factor[outer_pos][middle] * forward[middle]
        forward.append(partial_sum / factor[outer_pos][outer_pos])
    backward = [None for outer_pos in range(size_now)]
    for outer_pos in reversed(range(size_now)):
        partial_sum = forward[outer_pos]
        for middle in range(outer_pos + 1, size_now):
            partial_sum = partial_sum - factor[middle][outer_pos] * backward[middle]
        backward[outer_pos] = partial_sum / factor[outer_pos][outer_pos]
    return backward


def finish_kernel(place_ref, image_ref, *refs):
    known_refs, column_refs, out_ref, last_ref = refs[:KRYLOV], refs[KRYLOV : 2 * KRYLOV], refs[-2], refs[-1]
    orthogonalize(image_ref, known_refs, last_ref)
    norm = column_refs[0][0:1, :]
    columns = []
    for column, ref in enumerate(list(column_refs[1:]) + [last_ref]):
        columns.append([ref[i : i + 1, :] for i in range(column + 2)])
    gram = [
        [sum(columns[i][k] * columns[j][k] for k in range(j + 2)) for j in range(i + 1)]
        for i in range(KRYLOV)
    ]
    combination = small_solve(gram, [norm * columns[j][0] for j in range(KRYLOV)])
    piece_rows = out_ref.shape[0]
    part = pl.ds(pl.multiple_of(place_ref[0] * piece_rows, piece_rows), piece_rows)
    strengths = combination[0] * known_refs[0][part, :]
    for position in range(1, KRYLOV):
        strengths = strengths + combination[position] * known_refs[position][part, :]
    out_ref[...] = strengths


def finish(place, image, known, columns):
    piece_rows = image.shape[1]
    return pl.pallas_call(
        finish_kernel,
        out_shape=jax.ShapeDtypeStruct((piece_rows, LANES), jnp.float32),
        in_specs=[SMEM] + [VMEM] * (1 + len(known) + len(columns)),
        out_specs=VMEM,
        scratch_shapes=[pltpu.VMEM((8, LANES), jnp.float32)],
        compiler_params=pltpu.CompilerParams(vmem_limit_bytes=16 * 2**20),
        name="finish",
    )(place, image, *known, *columns)


def body(
    points,
    normals,
    freestream,
    wake_nodes,
    circulation,
    filament,
    self_term,
    near_blocks,
    near_index,
    far_left,
    far_right,
):
    everyone = ("wake", "col")
    n_wake, n_col = lax.axis_size("wake"), lax.axis_size("col")
    copies = n_wake * n_col
    piece = points.shape[1]
    piece_rows = piece // LANES
    mine = lax.axis_index("col")
    place = jnp.stack([lax.axis_index("wake") * n_col + mine, mine])

    near, index, left, right = near_blocks[:, 0, 0], near_index[:, 0, 0], far_left[0], far_right[0]
    dealt, rights = [], []
    for shift, part in enumerate(deal(place, index, near, left, n_col), 1):
        pairs = [(source, (source + shift) % n_col) for source in range(n_col)]
        dealt.append(lax.ppermute(part, "col", pairs))
        rights.append(lax.ppermute(right, "col", pairs))
    others = (dealt, rights)

    packed = pack_nodes(wake_nodes, circulation, filament, n_wake)
    panels = prepare_panels(points, normals, freestream)
    nodes = lax.all_to_all(packed, "wake", 0, 0, tiled=True)
    right_side, image_copies = induce(nodes, panels, copies)
    own_self = self_term.reshape(piece_rows, LANES)
    known, columns = [], []
    for _ in range(KRYLOV):
        image = lax.all_to_all(image_copies, everyone, 0, 0, tiled=True)
        (vector, column, image_copies), others = arnoldi_step(
            place, index, image, known, own_self, near, left, right, others
        )
        known.append(vector)
        columns.append(column)
    image = lax.all_to_all(image_copies, everyone, 0, 0, tiled=True)
    strengths = finish(place, image, known, columns)
    return right_side.reshape(piece), strengths.reshape(piece)


def solution(mesh):
    in_specs = (
        P(None, ("wake", "col")),
        P(None, ("wake", "col")),
        P(),
        P(None, "wake"),
        P("wake"),
        P("wake"),
        P(("wake", "col")),
        P("wake", "col", None, None, None),
        P("wake", "col", None),
        P("col", None, "wake"),
        P("wake", None, "col"),
    )
    out_specs = (P(("wake", "col")), P(("wake", "col")))
    return jax.shard_map(body, mesh=mesh, in_specs=in_specs, out_specs=out_specs, check_vma=False)
```

```python
import functools
import math

import jax
import jax.numpy as jnp
from jax import lax
from jax.experimental import pallas as pl
from jax.experimental.pallas import tpu as pltpu
from jax.sharding import PartitionSpec as P

KRYLOV = 6
CORE_SQ = 0.01
FOUR_PI = 4.0 * math.pi
LANES = 128
NORMAL_PRODUCTS = ((0, 0), (0, 1), (1, 0), (0, 2), (2, 0))
LENGTH_PRODUCTS = NORMAL_PRODUCTS + ((1, 1),)
FEATURES = 32
RUN = 4
DEPTH = FEATURES * RUN
WIDE = 2 * LANES
HALF = LANES // 2
BLOCKS = HALF // RUN
PANEL_STEP = 128
BLOCK_STEP = 16

VMEM = pl.BlockSpec(memory_space=pltpu.VMEM)
SMEM = pl.BlockSpec(memory_space=pltpu.SMEM)
HBM = pl.BlockSpec(memory_space=pltpu.HBM)


def pack_kernel(nodes_ref, circulation_ref, filament_ref, out_ref):
    copies, _, rows, _ = out_ref.shape
    own = [
        jnp.concatenate([nodes_ref[q : q + 1, r * LANES : (r + 1) * LANES] for r in range(rows)], axis=0)
        for q in range(3)
    ]
    own.append(circulation_ref[...])
    own.append(filament_ref[...].astype(jnp.float32) + 1.0)
    for q in range(5):
        for k in range(copies):
            out_ref[k, q] = own[q]


def pack_nodes(wake_nodes, circulation, filament, copies):
    rows = circulation.shape[0] // LANES
    return pl.pallas_call(
        pack_kernel,
        out_shape=jax.ShapeDtypeStruct((copies, 5, rows, LANES), jnp.float32),
        in_specs=[VMEM, VMEM, VMEM],
        out_specs=VMEM,
        name="pack_nodes",
    )(wake_nodes, circulation.reshape(rows, LANES), filament.reshape(rows, LANES))


def three_pieces(value):
    high = value.astype(jnp.bfloat16).astype(jnp.float32)
    rest = value - high
    middle = rest.astype(jnp.bfloat16).astype(jnp.float32)
    low = (rest - middle).astype(jnp.bfloat16).astype(jnp.float32)
    return high, middle, low


def panels_kernel(
    points_ref, normals_ref, stream_ref, normal_side_out, length_side_out, info_out,
    normal_side_ref, length_side_ref, info_ref, left,
):
    piece_rows = info_ref.shape[0] - 8

    def spread(ref, q):
        return jnp.concatenate(
            [ref[q : q + 1, r * LANES : (r + 1) * LANES] for r in range(piece_rows)], axis=0
        )

    points = [spread(points_ref, q) for q in range(3)]
    normals = [spread(normals_ref, q) for q in range(3)]
    middle = [0.5 * (jnp.max(p, keepdims=True) + jnp.min(p, keepdims=True)) for p in points]
    info_ref[...] = jnp.zeros_like(info_ref)
    info_ref[0:piece_rows, :] = (
        stream_ref[0] * normals[0] + stream_ref[1] * normals[1] + stream_ref[2] * normals[2]
    )
    for q in range(3):
        info_ref[piece_rows + q : piece_rows + q + 1, :] = jnp.broadcast_to(middle[q], (1, LANES))
    px, py, pz = [points[q] - middle[q] for q in range(3)]
    features = [
        normals[1] * pz - normals[2] * py,
        normals[2] * px - normals[0] * pz,
        normals[0] * py - normals[1] * px,
        normals[0], normals[1], normals[2],
    ]
    blank = jnp.zeros_like(px)
    pieces = [three_pieces(feature) for feature in features]
    side = [pieces[k][p] for p, _ in NORMAL_PRODUCTS for k in range(6)]
    side += [blank] * (FEATURES - len(side))
    pieces = [three_pieces(value) for value in (px, py, pz)]
    side += [pieces[k][p] for p, _ in LENGTH_PRODUCTS for k in range(3)]
    side += list(three_pieces(px * px + py * py + pz * pz)) + [jnp.ones_like(px)] * 3
    side += [blank] * (LANES - len(side))
    column = lax.broadcasted_iota(jnp.int32, (FEATURES, DEPTH), 1)
    first = lax.broadcasted_iota(jnp.int32, (FEATURES, DEPTH), 0) * RUN
    again = jnp.where((column >= first) & (column < first + RUN), 1.0, 0.0).astype(jnp.bfloat16)
    for r in range(piece_rows):
        own = slice(r * LANES, (r + 1) * LANES)
        turned = jnp.concatenate([value[r : r + 1, :] for value in side], axis=0).T.astype(jnp.bfloat16)
        for ref, start in ((normal_side_ref, 0), (length_side_ref, FEATURES)):
            wide = jnp.dot(turned[:, start : start + FEATURES], again, preferred_element_type=jnp.float32)
            ref[own, :] = wide.astype(jnp.bfloat16)
    leaving = [
        pltpu.make_async_copy(source, target, left.at[i])
        for i, (source, target) in enumerate(
            (
                (normal_side_ref, normal_side_out),
                (length_side_ref, length_side_out),
                (info_ref, info_out),
            )
        )
    ]
    for copy in leaving:
        copy.start()
    for copy in leaving:
        copy.wait()


def prepare_panels(points, normals, freestream):
    piece = points.shape[1]
    return pl.pallas_call(
        panels_kernel,
        out_shape=(
            jax.ShapeDtypeStruct((piece, DEPTH), jnp.bfloat16),
            jax.ShapeDtypeStruct((piece, DEPTH), jnp.bfloat16),
            jax.ShapeDtypeStruct((piece // LANES + 8, LANES), jnp.float32),
        ),
        in_specs=[VMEM, VMEM, SMEM],
        out_specs=(HBM, HBM, HBM),
        scratch_shapes=[
            pltpu.VMEM((piece, DEPTH), jnp.bfloat16),
            pltpu.VMEM((piece, DEPTH), jnp.bfloat16),
            pltpu.VMEM((piece // LANES + 8, LANES), jnp.float32),
            pltpu.SemaphoreType.DMA((3,)),
        ],
        name="prepare_panels",
    )(points, normals, freestream)


def induce_kernel(
    nodes_in, normal_side_in, length_side_in, info_in, right_ref, copies_ref,
    nodes_ref, normal_side_ref, length_side_ref, info_ref,
    normal_ref, length_ref, square_ref, normal_pick_ref, length_pick_ref, total_ref, arrived,
):
    fetches = [
        pltpu.make_async_copy(source, target, arrived.at[i])
        for i, (source, target) in enumerate(
            (
                (nodes_in, nodes_ref),
                (info_in, info_ref),
                (normal_side_in, normal_side_ref),
                (length_side_in, length_side_ref),
            )
        )
    ]
    for fetch in fetches:
        fetch.start()
    fetches[0].wait()
    fetches[1].wait()
    rows = nodes_ref.shape[0] * nodes_ref.shape[2]
    groups = rows // LANES
    x, y, z, circulation, tag = [nodes_ref[:, q].reshape(rows, LANES) for q in range(5)]
    piece_rows = right_ref.shape[0]
    lane = lax.broadcasted_iota(jnp.int32, (rows, LANES), 1)
    row = lax.broadcasted_iota(jnp.int32, (rows, LANES), 0)
    turned = pltpu.roll(tag, LANES - 1, 1)
    next_tag = jnp.where(lane == LANES - 1, pltpu.roll(turned, rows - 1, 0), turned)
    linked = (tag == next_tag) & ((lane < LANES - 1) | (row < rows - 1))
    strength = jnp.where(linked, circulation * (2.0 / FOUR_PI), 0.0)
    runs = [
        [
            (value - info_ref[piece_rows + q : piece_rows + q + 1, :])[g * LANES : (g + 1) * LANES].T
            for q, value in enumerate((x, y, z))
        ]
        for g in range(groups)
    ]
    total_ref[...] = jnp.zeros_like(total_ref)
    last = lax.broadcasted_iota(jnp.int32, (1, LANES), 1) == LANES - 1
    blank = jnp.zeros((LANES, LANES), jnp.float32)
    ones = jnp.ones((LANES, LANES), jnp.float32)

    def put(ref, features, blocks, to=0):
        features = features + [blank] * (FEATURES - len(features))
        count = 16 // RUN
        for k in range(0, FEATURES, count):
            for half in range(2):
                for block in range(blocks):
                    start = half * HALF + block * RUN
                    rows = jnp.concatenate([value[start : start + RUN] for value in features[k : k + count]], axis=0)
                    ref[to + block, k * RUN : (k + count) * RUN, half * LANES : (half + 1) * LANES] = rows.astype(
                        jnp.bfloat16
                    )

    for group in range(groups):
        a = runs[group]
        b = []
        for q in range(3):
            end = jnp.where(
                last, runs[(group + 1) % groups][q][0:1, 0:1], pltpu.roll(a[q][0:1, :], LANES - 1, 1)
            )
            b.append(jnp.concatenate([a[q][1:], end], axis=0))
        g = strength[group * LANES : (group + 1) * LANES].T
        ends = [g * (a[q] - b[q]) for q in range(3)]
        ends += [
            g * (a[1] * b[2] - a[2] * b[1]),
            g * (a[2] * b[0] - a[0] * b[2]),
            g * (a[0] * b[1] - a[1] * b[0]),
        ]
        pieces = [three_pieces(value) for value in ends]
        put(normal_ref, [pieces[k][p] for _, p in NORMAL_PRODUCTS for k in range(6)], BLOCKS)

        def length_rows(linear, square):
            pieces = [three_pieces(value) for value in linear]
            rows = [pieces[k][p] for _, p in LENGTH_PRODUCTS for k in range(3)]
            return rows + [ones] * 3 + list(three_pieces(square))

        square = sum((a[q] - b[q]) * (a[q] - b[q]) for q in range(3))
        for half in range(2):
            square_ref[:, half * LANES : (half + 1) * LANES] = square[half * HALF : (half + 1) * HALF]
        after = length_rows([-2.0 * b[q] for q in range(3)], b[0] * b[0] + b[1] * b[1] + b[2] * b[2])
        put(length_ref, after, BLOCKS)
        start = length_rows([-2.0 * a[q] for q in range(3)], a[0] * a[0] + a[1] * a[1] + a[2] * a[2])
        put(length_ref, start, 1, BLOCKS)
        if group == 0:
            fetches[2].wait()
            fetches[3].wait()

        def panel_step(b, carry):
            part = pl.ds(pl.multiple_of(b * PANEL_STEP, PANEL_STEP), PANEL_STEP)
            place = lax.broadcasted_iota(jnp.int32, (1, DEPTH), 1) % RUN
            for j in range(RUN):
                mask = jnp.where(place == j, 1.0, 0.0).astype(jnp.bfloat16)
                normal_pick_ref[j] = normal_side_ref[part, :] * mask
                length_pick_ref[j] = length_side_ref[part, :] * mask

            def form(pick_ref, j, weights):
                return jnp.dot(pick_ref[j], weights, preferred_element_type=jnp.float32)

            def length_of(square):
                square = jnp.maximum(square, 1e-30)
                return square * lax.rsqrt(square)

            def node_step(step, state):
                length, total = state
                for i in range(BLOCK_STEP):
                    block = step * BLOCK_STEP + i
                    for j in range(RUN):
                        normal_part = form(normal_pick_ref, j, normal_ref[block])
                        after = length_of(form(length_pick_ref, j, length_ref[block]))
                        reach = length + after
                        gap = reach * reach - square_ref[pl.ds(block * RUN + j, 1), :]
                        below = (length * after) * gap + 2.0 * CORE_SQ
                        total = total + (reach * normal_part) * pl.reciprocal(below)
                        length = after
                return length, total

            start = (
                length_of(form(length_pick_ref, 0, length_ref[BLOCKS])),
                jnp.zeros((PANEL_STEP, WIDE), jnp.float32),
            )
            _, total = lax.fori_loop(0, BLOCKS // BLOCK_STEP, node_step, start)
            total_ref[part, :] += total[:, :LANES] + total[:, LANES:]
            return carry

        lax.fori_loop(0, piece_rows * LANES // PANEL_STEP, panel_step, 0)

    for r in range(piece_rows):
        induced = jnp.sum(total_ref[r * LANES : (r + 1) * LANES, :].T, axis=0, keepdims=True)
        right_ref[r : r + 1, :] = -(info_ref[r : r + 1, :] + induced)
    right = right_ref[...]
    for k in range(copies_ref.shape[0]):
        copies_ref[k] = right


def induce(nodes, panels, copies):
    piece = panels[0].shape[0]
    piece_rows = piece // LANES
    pairs = piece * nodes.size // 5
    return pl.pallas_call(
        induce_kernel,
        out_shape=(
            jax.ShapeDtypeStruct((piece_rows, LANES), jnp.float32),
            jax.ShapeDtypeStruct((copies, piece_rows, LANES), jnp.float32),
        ),
        in_specs=[HBM] * 4,
        out_specs=(VMEM, VMEM),
        scratch_shapes=[
            pltpu.VMEM(nodes.shape, jnp.float32),
            pltpu.VMEM((piece, DEPTH), jnp.bfloat16),
            pltpu.VMEM((piece, DEPTH), jnp.bfloat16),
            pltpu.VMEM((piece_rows + 8, LANES), jnp.float32),
            pltpu.VMEM((BLOCKS, DEPTH, WIDE), jnp.bfloat16),
            pltpu.VMEM((BLOCKS + 1, DEPTH, WIDE), jnp.bfloat16),
            pltpu.VMEM((HALF, WIDE), jnp.float32),
            pltpu.VMEM((RUN, PANEL_STEP, DEPTH), jnp.bfloat16),
            pltpu.VMEM((RUN, PANEL_STEP, DEPTH), jnp.bfloat16),
            pltpu.VMEM((piece, LANES), jnp.float32),
            pltpu.SemaphoreType.DMA((4,)),
        ],
        compiler_params=pltpu.CompilerParams(vmem_limit_bytes=60 * 2**20),
        cost_estimate=pl.CostEstimate(flops=30 * pairs, bytes_accessed=2**21, transcendentals=2 * pairs),
        name="induce",
    )(nodes, *panels)


def whole_sum(value):
    return jnp.sum(value, keepdims=True)


def orthogonalize(image_ref, known_refs, column_ref):
    image = image_ref[...].reshape(-1, LANES)
    known = [ref[...] for ref in known_refs]
    coeffs = [whole_sum(image * member) for member in known]
    for coeff, member in zip(coeffs, known):
        image = image - coeff * member
    norm = jnp.sqrt(whole_sum(image * image))
    for i, value in enumerate(coeffs + [norm]):
        column_ref[i : i + 1, :] = jnp.broadcast_to(value, (1, LANES))
    return image / norm


def deal_kernel(place_ref, index_ref, near_ref, left_ref, *out_refs):
    n_col = len(out_refs) + 1
    rank, width = left_ref.shape
    piece_rows = width // LANES // n_col
    lane = lax.broadcasted_iota(jnp.int32, (8, LANES), 1)
    for shift in range(1, n_col):
        out_ref = out_refs[shift - 1]
        first = lax.rem(place_ref[1] + shift, n_col) * piece_rows
        index = jnp.zeros((8, LANES), jnp.float32)
        for r in range(piece_rows):
            base = r * (LANES + rank)
            out_ref[base : base + LANES, :] = near_ref[first + r]
            columns = pl.ds(pl.multiple_of((first + r) * LANES, LANES), LANES)
            out_ref[base + LANES : base + LANES + rank, :] = left_ref[:, columns]
            index = jnp.where(lane == r, index_ref[first + r].astype(jnp.float32), index)
        out_ref[piece_rows * (LANES + rank) :, :] = index


def deal(place, index, near, left, n_col):
    rank, width = left.shape
    piece_rows = width // LANES // n_col
    shape = jax.ShapeDtypeStruct((piece_rows * (LANES + rank) + 8, LANES), jnp.float32)
    return pl.pallas_call(
        deal_kernel,
        out_shape=(shape,) * (n_col - 1),
        in_specs=[SMEM, SMEM, VMEM, VMEM],
        out_specs=(VMEM,) * (n_col - 1),
        compiler_params=pltpu.CompilerParams(vmem_limit_bytes=16 * 2**20),
        name="deal",
    )(place, index, near, left)


def step_kernel(known_count, n_col, opening, *refs):
    place_ref, own_index_ref, refs = refs[0], refs[1], refs[2:]
    other = n_col - 1
    index_refs, refs = (None, refs) if opening else (refs[:other], refs[other:])
    image_ref, known_refs, refs = refs[0], refs[1 : 1 + known_count], refs[1 + known_count :]
    self_ref, near_ref, left_ref, right_ref, refs = refs[0], refs[1], refs[2], refs[3], refs[4:]
    dealt_refs, right_refs, refs = refs[:other], refs[other : 2 * other], refs[2 * other :]
    vector_ref, column_ref, copies_ref = refs[:3]
    fetches = []
    if opening:
        dealt_in, right_in = dealt_refs, right_refs
        refs = refs[3:]
        index_refs, dealt_refs, right_refs = refs[:other], refs[other : 2 * other], refs[2 * other : 3 * other]
        arrived = refs[3 * other]
        for i, (source, target) in enumerate(
            list(zip(dealt_in, dealt_refs)) + list(zip(right_in, right_refs))
        ):
            fetches.append(pltpu.make_async_copy(source, target, arrived.at[i]))
            fetches[-1].start()
    piece_rows = self_ref.shape[0]
    piece = piece_rows * LANES
    rank = right_ref.shape[0]
    n_wake = right_ref.shape[1] // piece
    vector_ref[...] = orthogonalize(image_ref, known_refs, column_ref)
    place, mine = place_ref[0], place_ref[1]
    for fetch in fetches:
        fetch.wait()
    if opening:
        lane = lax.broadcasted_iota(jnp.int32, (1, LANES), 1)
        for index_ref, dealt_ref in zip(index_refs, dealt_refs):
            last = dealt_ref.shape[0] - 8
            row = dealt_ref[last : last + 1, :]
            for r in range(piece_rows):
                index_ref[r] = jnp.sum(jnp.where(lane == r, row, 0.0)).astype(jnp.int32)
    index_refs = (own_index_ref, *index_refs)
    right_refs = (right_ref, *right_refs)

    far = [jnp.zeros((rank, LANES), jnp.float32) for _ in range(piece_rows)]
    near = [jnp.zeros((LANES, LANES), jnp.float32) for _ in range(piece_rows)]
    for shift in range(n_col):
        group = lax.rem(mine - shift + n_col, n_col)

        def chunk(w, total):
            first = (w * n_col + group) * piece_rows
            for r in range(piece_rows):
                entries = vector_ref[pl.ds(first + r, 1), :]
                columns = pl.ds(pl.multiple_of(w * piece, LANES) + r * LANES, LANES)
                total = total + right_refs[shift][:, columns] * entries
            return total

        coeff = lax.fori_loop(0, n_wake, chunk, jnp.zeros((rank, LANES), jnp.float32), unroll=4)
        coeff = jnp.sum(coeff, axis=1, keepdims=True)
        for r in range(piece_rows):
            if shift == 0:
                row_block = mine * piece_rows + r
                block = index_refs[0][row_block]
                left = left_ref[:, pl.ds(pl.multiple_of(row_block * LANES, LANES), LANES)]
                matrix = near_ref[row_block]
            else:
                base = r * (LANES + rank)
                block = index_refs[shift][r]
                left = dealt_refs[shift - 1][base + LANES : base + LANES + rank, :]
                matrix = dealt_refs[shift - 1][base : base + LANES, :]
            where = (lax.div(block, piece_rows) * n_col + group) * piece_rows + lax.rem(block, piece_rows)
            far[r] = far[r] + left * coeff
            near[r] = near[r] + matrix * vector_ref[pl.ds(where, 1), :]
    image = jnp.concatenate(
        [
            jnp.sum(near[r].T, axis=0, keepdims=True) + jnp.sum(far[r], axis=0, keepdims=True)
            for r in range(piece_rows)
        ],
        axis=0,
    )
    own = vector_ref[pl.ds(pl.multiple_of(place * piece_rows, piece_rows), piece_rows), :]
    image = self_ref[...] * own + image
    for k in range(copies_ref.shape[0]):
        copies_ref[k] = image


def arnoldi_step(place, index, image, known, self_term, near, left, right, others):
    copies, piece_rows, _ = image.shape
    opening = len(known) == 0
    dealt, rights = others[-2:]
    out_shape = [
        jax.ShapeDtypeStruct((copies * piece_rows, LANES), jnp.float32),
        jax.ShapeDtypeStruct((8, LANES), jnp.float32),
        jax.ShapeDtypeStruct((copies, piece_rows, LANES), jnp.float32),
    ]
    out_specs, scratch = [VMEM] * 3, []
    indices = [] if opening else others[0]
    operands = [image, *known, self_term, near, left, right]
    in_specs = [SMEM] * (2 + len(indices)) + [VMEM] * len(operands)
    in_specs += [HBM if opening else VMEM] * (len(dealt) + len(rights))
    if opening:
        out_shape += [jax.ShapeDtypeStruct((piece_rows,), jnp.int32) for _ in dealt]
        out_shape += [jax.ShapeDtypeStruct(value.shape, jnp.float32) for value in (*dealt, *rights)]
        out_specs += [SMEM] * len(dealt) + [VMEM] * (len(dealt) + len(rights))
        scratch = [pltpu.SemaphoreType.DMA((max(1, len(dealt) + len(rights)),))]
    results = pl.pallas_call(
        functools.partial(step_kernel, len(known), 1 + len(dealt), opening),
        out_shape=tuple(out_shape),
        in_specs=in_specs,
        out_specs=tuple(out_specs),
        scratch_shapes=scratch,
        compiler_params=pltpu.CompilerParams(vmem_limit_bytes=24 * 2**20),
        name="arnoldi_step",
    )(place, index, *indices, *operands, *dealt, *rights)
    if opening:
        count = len(dealt)
        rest = results[3:]
        others = (rest[:count], rest[count : 2 * count], rest[2 * count :])
    return results[:3], others


def small_solve(gram_matrix, projected):
    size_now = len(projected)
    factor = [[None for inner_pos in range(size_now)] for outer_pos in range(size_now)]
    for outer_pos in range(size_now):
        for inner_pos in range(outer_pos + 1):
            partial_sum = gram_matrix[outer_pos][inner_pos]
            for middle in range(inner_pos):
                partial_sum = partial_sum - factor[outer_pos][middle] * factor[inner_pos][middle]
            if inner_pos == outer_pos:
                factor[outer_pos][inner_pos] = jnp.sqrt(partial_sum)
            else:
                factor[outer_pos][inner_pos] = partial_sum / factor[inner_pos][inner_pos]
    forward = []
    for outer_pos in range(size_now):
        partial_sum = projected[outer_pos]
        for middle in range(outer_pos):
            partial_sum = partial_sum - factor[outer_pos][middle] * forward[middle]
        forward.append(partial_sum / factor[outer_pos][outer_pos])
    backward = [None for outer_pos in range(size_now)]
    for outer_pos in reversed(range(size_now)):
        partial_sum = forward[outer_pos]
        for middle in range(outer_pos + 1, size_now):
            partial_sum = partial_sum - factor[middle][outer_pos] * backward[middle]
        backward[outer_pos] = partial_sum / factor[outer_pos][outer_pos]
    return backward


def finish_kernel(place_ref, image_ref, *refs):
    known_refs, column_refs, out_ref, last_ref = refs[:KRYLOV], refs[KRYLOV : 2 * KRYLOV], refs[-2], refs[-1]
    orthogonalize(image_ref, known_refs, last_ref)
    norm = column_refs[0][0:1, :]
    columns = []
    for column, ref in enumerate(list(column_refs[1:]) + [last_ref]):
        columns.append([ref[i : i + 1, :] for i in range(column + 2)])
    gram = [
        [sum(columns[i][k] * columns[j][k] for k in range(j + 2)) for j in range(i + 1)]
        for i in range(KRYLOV)
    ]
    combination = small_solve(gram, [norm * columns[j][0] for j in range(KRYLOV)])
    piece_rows = out_ref.shape[0]
    part = pl.ds(pl.multiple_of(place_ref[0] * piece_rows, piece_rows), piece_rows)
    strengths = combination[0] * known_refs[0][part, :]
    for position in range(1, KRYLOV):
        strengths = strengths + combination[position] * known_refs[position][part, :]
    out_ref[...] = strengths


def finish(place, image, known, columns):
    piece_rows = image.shape[1]
    return pl.pallas_call(
        finish_kernel,
        out_shape=jax.ShapeDtypeStruct((piece_rows, LANES), jnp.float32),
        in_specs=[SMEM] + [VMEM] * (1 + len(known) + len(columns)),
        out_specs=VMEM,
        scratch_shapes=[pltpu.VMEM((8, LANES), jnp.float32)],
        compiler_params=pltpu.CompilerParams(vmem_limit_bytes=16 * 2**20),
        name="finish",
    )(place, image, *known, *columns)


def body(
    points,
    normals,
    freestream,
    wake_nodes,
    circulation,
    filament,
    self_term,
    near_blocks,
    near_index,
    far_left,
    far_right,
):
    everyone = ("wake", "col")
    n_wake, n_col = lax.axis_size("wake"), lax.axis_size("col")
    copies = n_wake * n_col
    piece = points.shape[1]
    piece_rows = piece // LANES
    mine = lax.axis_index("col")
    place = jnp.stack([lax.axis_index("wake") * n_col + mine, mine])

    near, index, left, right = near_blocks[:, 0, 0], near_index[:, 0, 0], far_left[0], far_right[0]
    packed, sent = lax.optimization_barrier((pack_nodes(wake_nodes, circulation, filament, n_wake), right))
    dealt, rights = [], []
    for shift, part in enumerate(deal(place, index, near, left, n_col), 1):
        pairs = [(source, (source + shift) % n_col) for source in range(n_col)]
        dealt.append(lax.ppermute(part, "col", pairs))
        rights.append(lax.ppermute(sent, "col", pairs))
    others = (dealt, rights)

    panels = prepare_panels(points, normals, freestream)
    nodes = lax.all_to_all(packed, "wake", 0, 0, tiled=True)
    right_side, image_copies = induce(nodes, panels, copies)
    own_self = self_term.reshape(piece_rows, LANES)
    known, columns = [], []
    for _ in range(KRYLOV):
        image = lax.all_to_all(image_copies, everyone, 0, 0, tiled=True)
        (vector, column, image_copies), others = arnoldi_step(
            place, index, image, known, own_self, near, left, right, others
        )
        known.append(vector)
        columns.append(column)
    image = lax.all_to_all(image_copies, everyone, 0, 0, tiled=True)
    strengths = finish(place, image, known, columns)
    return right_side.reshape(piece), strengths.reshape(piece)


def solution(mesh):
    in_specs = (
        P(None, ("wake", "col")),
        P(None, ("wake", "col")),
        P(),
        P(None, "wake"),
        P("wake"),
        P("wake"),
        P(("wake", "col")),
        P("wake", "col", None, None, None),
        P("wake", "col", None),
        P("col", None, "wake"),
        P("wake", None, "col"),
    )
    out_specs = (P(("wake", "col")), P(("wake", "col")))
    return jax.shard_map(body, mesh=mesh, in_specs=in_specs, out_specs=out_specs, check_vma=False)
```
